32 devices in a mesh: groups: 2 (over x), blk: 16 (over z, y, core).
Axes of the slice: x: 2, y: 2, z: 4, core: 2. Of those that a mesh axis runs over, the one named last changes fastest.
Arguments:
- queries: bfloat16 [32, 8192], P(('groups', 'blk')), parts along dimension 0, may hold values from -100 to 100
- prefix_key_value: bfloat16 [2, 32768, 1024], P(None, ('groups', 'blk')), parts along dimension 1, may hold values from -7 to 7
- suffix_key_value: bfloat16 [32, 2, 512, 1024], P(('groups', 'blk')), parts along dimension 0, may hold values from -9 to 9
- fresh_key_value: bfloat16 [32, 2, 1024], P(('groups', 'blk')), parts along dimension 0, may hold values from -9 to 9
- lengths: int32 [32], P('groups'), parts along dimension 0, may hold values from 1 to 512, 4096 in all
- home: int32 [32], P('groups'), parts along dimension 0, may hold values from 0 to 15, each once
Outputs:
- attended: bfloat16 [32, 8192], P(('groups', 'blk')), parts along dimension 0
The draws below stay inside these ranges and needn't reach their ends.
There are 2 independent parts, one for each index of `groups`. The reference program is written for one: setup_inputs(seed, part) draws one part's arguments, and reference() takes and returns one part's arrays. A program takes and returns all parts, laid end to end along the dimension named above; each array names one. Nothing has to cross between parts.
Inputs may be any that keep to these rules, and one draw needn't show every extreme that they name: Row r's suffix cache lies in slot home[r]; every slot holds exactly one row. `lengths`: some row has exactly 512 suffix tokens.
All inputs are finite; a program needn't handle non-finite values.
Results may differ from the reference program's by a relative error of at most 0.0049.
Values may be sent and summed in bfloat16 or wider, within the bound.
A program may use at most 128 MiB of HBM per device.

```python
import math
import jax
import jax.numpy as jnp
import numpy as np
from jax import lax

QUERY_HEADS = 64
KEY_VALUE_HEADS = 8
HEAD_WIDTH = 128
ROWS_DEV = 1
PREFIX_PER_BLOCK = 1024
SUFFIX_SLOTS = 512
REVISION_ROWS = 16
PREFIX_TOTAL = 16384
N_BLK = 16


def prefix_stream(random_seed_key):
    table_entries = jax.random.normal(jax.random.fold_in(random_seed_key, 11), (2, PREFIX_TOTAL, KEY_VALUE_HEADS * HEAD_WIDTH), jnp.float32)
    table_entries = jnp.clip(table_entries, -6.0, 6.0)
    return table_entries


def draw_prefix_key_value(key, part):
    table_entries = prefix_stream(key)
    return table_entries.astype(jnp.bfloat16)


def draw_queries(key, part):
    base = 3.0 * jax.random.normal(jax.random.fold_in(key, 21), (REVISION_ROWS, QUERY_HEADS * HEAD_WIDTH), jnp.float32)
    base = jnp.clip(base, -100.0, 100.0)
    return base.astype(jnp.bfloat16)


def level_of(own_key, dims, cuts, least, high):
    factor_of = 1.0
    for position, blocks in cuts:
        steps = jax.random.uniform(jax.random.fold_in(jax.random.fold_in(own_key, 6), position), (blocks,), jnp.float32, least / len(cuts), high / len(cuts))
        factor_of = factor_of * jnp.repeat(jnp.exp(steps), dims[position] // blocks).reshape((-1,) + (1,) * (len(dims) - 1 - position))
    return factor_of


def split_up(number_of, total, bound, skew):
    portions = [(1 << 20) // math.isqrt(standing ** skew) + 1 for standing in range(2, number_of + 1)]
    rest, given = total - bound - (number_of - 1), [1] * (number_of - 1)
    while rest > 0:
        free = [i for i in range(number_of - 1) if given[i] < bound]
        whole, remaining = sum([portions[i] for i in free]), rest
        for i in free:
            extra = min(bound - given[i], max(1, remaining * portions[i] // whole), rest)
            given[i] = given[i] + extra
            rest = rest - extra
    return np.array([bound] + given)


def uneven_parts(rng, count, total, bound, lean):
    if count == 2:
        one = jax.random.randint(rng, (), max(1, total - bound), min(bound, total - 1) + 1)
        return jnp.stack([one, total - one])
    sizes = jnp.asarray(split_up(count, total, bound, lean), jnp.int32)
    couples = (count - 1) // 2
    giver, taker = sizes[1:1 + 2 * couples:2], sizes[2:2 + 2 * couples:2]
    margin = jnp.minimum(giver - 1, bound - taker)
    shifted = jax.random.randint(jax.random.fold_in(rng, 1), (couples,), 0, 1 << 20) % (margin + 1)
    sizes = sizes.at[1:1 + 2 * couples:2].set(giver - shifted).at[2:2 + 2 * couples:2].set(taker + shifted)
    return sizes[jax.random.permutation(jax.random.fold_in(rng, 2), count)]


def centred(rng, extent, spread, bound, split=(), held_as=jnp.bfloat16):
    level = level_of(rng, extent, split, -0.22, 0.18) if split else 1.0
    values = jax.random.normal(rng, extent, jnp.float32) * spread * level
    return jnp.minimum(jnp.maximum(values, -bound), bound).astype(held_as)


def setup_inputs(seed: int = 0, part: int = 0) -> dict:
    seeds = jax.random.split(jax.random.key(seed), 7)
    own_keys = jax.random.split(jax.random.fold_in(seeds[6], part), 7)
    queries = draw_queries(jax.random.fold_in(jax.random.fold_in(seeds[6], part), 71), part)
    prefix_key_value = draw_prefix_key_value(jax.random.fold_in(jax.random.fold_in(seeds[6], part), 71), part)
    suffix_key_value = centred(own_keys[2], (REVISION_ROWS, 2, SUFFIX_SLOTS, KEY_VALUE_HEADS * HEAD_WIDTH), 1.5, 9.0, ((0, 16),))
    fresh_key_value = centred(own_keys[3], (REVISION_ROWS, 2, KEY_VALUE_HEADS * HEAD_WIDTH), 1.5, 9.0, ((0, 16),))
    lengths = uneven_parts(own_keys[4], REVISION_ROWS, REVISION_ROWS * SUFFIX_SLOTS // 2, SUFFIX_SLOTS, 2).astype(jnp.int32)
    home = jax.random.permutation(own_keys[5], REVISION_ROWS).astype(jnp.int32)
    return {"queries": queries, "prefix_key_value": prefix_key_value, "suffix_key_value": suffix_key_value, "fresh_key_value": fresh_key_value, "lengths": lengths, "home": home}


def part_stats(scores, values):
    peak = jnp.max(scores, axis=-1)
    exponent = jnp.exp(scores - peak[..., None])
    totals = jnp.sum(exponent, axis=-1)
    weights = exponent.astype(jnp.bfloat16).astype(jnp.float32)
    accum = jnp.einsum("rhgt,rthd->rhgd", weights, values)
    return peak, totals, accum


def reference(queries, prefix_key_value, suffix_key_value, fresh_key_value, lengths, home):
    query_group = QUERY_HEADS // KEY_VALUE_HEADS
    score_scale = HEAD_WIDTH ** -0.5
    query_head_rows = queries.reshape(REVISION_ROWS, KEY_VALUE_HEADS, query_group, HEAD_WIDTH).astype(jnp.float32)

    def suffix_row(item):
        query_row, slot_id, length = item
        cache_tile_index = lax.dynamic_index_in_dim(suffix_key_value, slot_id, 0, keepdims=False)
        row_key_slice = cache_tile_index[0].reshape(SUFFIX_SLOTS, KEY_VALUE_HEADS, HEAD_WIDTH).astype(jnp.float32)
        row_value_slice = cache_tile_index[1].reshape(SUFFIX_SLOTS, KEY_VALUE_HEADS, HEAD_WIDTH).astype(jnp.float32)
        scores = jnp.einsum("hgd,thd->hgt", query_row, row_key_slice) * score_scale
        live_mask = jnp.arange(SUFFIX_SLOTS, dtype=jnp.int32) < length
        scores = jnp.where(live_mask[None, None, :], scores, -jnp.inf)
        peak, totals, accum = part_stats(scores[None], row_value_slice[None])
        return peak[0], totals[0], accum[0]

    suffix_score_peak, suffix_weight_sum, suffix_accum_sum = lax.map(suffix_row, (query_head_rows, home, lengths))
    fresh_token_keys = fresh_key_value[:, 0].reshape(REVISION_ROWS, KEY_VALUE_HEADS, HEAD_WIDTH).astype(jnp.float32)
    fresh_token_values = fresh_key_value[:, 1].reshape(REVISION_ROWS, KEY_VALUE_HEADS, HEAD_WIDTH).astype(jnp.float32)
    new_peak = jnp.einsum("rhgd,rhd->rhg", query_head_rows, fresh_token_keys) * score_scale
    new_total = jnp.ones_like(new_peak)
    fresh_token_accum = jnp.broadcast_to(fresh_token_values[:, :, None, :], (REVISION_ROWS, KEY_VALUE_HEADS, query_group, HEAD_WIDTH))
    row_ids = jnp.arange(REVISION_ROWS, dtype=jnp.int32)

    def block_step(carry, block_id):
        run_peak, run_num, run_den = carry
        start_offset = (block_id * PREFIX_PER_BLOCK).astype(jnp.int32)
        cache_tile_index = lax.dynamic_slice_in_dim(prefix_key_value, start_offset, PREFIX_PER_BLOCK, 1)
        block_key_rows = cache_tile_index[0].reshape(PREFIX_PER_BLOCK, KEY_VALUE_HEADS, HEAD_WIDTH).astype(jnp.float32)
        block_value_rows = cache_tile_index[1].reshape(PREFIX_PER_BLOCK, KEY_VALUE_HEADS, HEAD_WIDTH).astype(jnp.float32)
        scores = jnp.einsum("rhgd,thd->rhgt", query_head_rows, block_key_rows) * score_scale
        prefix_score_peak = jnp.max(scores, axis=-1)
        exponent = jnp.exp(scores - prefix_score_peak[..., None])
        prefix_weight_sum = jnp.sum(exponent, axis=-1)
        weights = exponent.astype(jnp.bfloat16).astype(jnp.float32)
        prefix_accum_sum = jnp.einsum("rhgt,thd->rhgd", weights, block_value_rows)
        suf_here = (home // ROWS_DEV == block_id)[:, None, None]
        new_here = (row_ids // ROWS_DEV == block_id)[:, None, None]
        suf_peak_b = jnp.where(suf_here, suffix_score_peak, -jnp.inf)
        new_peak_b = jnp.where(new_here, new_peak, -jnp.inf)
        peak = jnp.maximum(prefix_score_peak, jnp.maximum(suf_peak_b, new_peak_b))
        pre_fac = jnp.exp(prefix_score_peak - peak)
        suf_fac = jnp.where(suf_here, jnp.exp(suf_peak_b - peak), 0.0)
        new_fac = jnp.where(new_here, jnp.exp(new_peak_b - peak), 0.0)
        totals = pre_fac * prefix_weight_sum + suf_fac * suffix_weight_sum + new_fac * new_total
        accum = pre_fac[..., None] * prefix_accum_sum + suf_fac[..., None] * suffix_accum_sum + new_fac[..., None] * fresh_token_accum
        normed = (accum / totals[..., None]).astype(jnp.bfloat16)
        normed = lax.optimization_barrier(normed).astype(jnp.float32)
        lse = peak + jnp.log(totals)
        next_peak = jnp.maximum(run_peak, lse)
        old_fac = jnp.exp(run_peak - next_peak)
        blk_fac = jnp.exp(lse - next_peak)
        run_num = run_num * old_fac[..., None] + blk_fac[..., None] * normed
        run_den = run_den * old_fac + blk_fac
        return (next_peak, run_num, run_den), None

    initial_carry = (jnp.full((REVISION_ROWS, KEY_VALUE_HEADS, query_group), -jnp.inf, jnp.float32),
                   jnp.zeros((REVISION_ROWS, KEY_VALUE_HEADS, query_group, HEAD_WIDTH), jnp.float32),
                   jnp.zeros((REVISION_ROWS, KEY_VALUE_HEADS, query_group), jnp.float32))
    final, _ = lax.scan(block_step, initial_carry, jnp.arange(N_BLK, dtype=jnp.int32))
    result = final[1] / final[2][..., None]
    return result.reshape(REVISION_ROWS, QUERY_HEADS * HEAD_WIDTH).astype(jnp.bfloat16)
```

```python
import functools

import jax
import jax.numpy as jnp
from jax import lax
from jax.experimental import pallas as pl
from jax.experimental.pallas import tpu as pltpu
from jax.sharding import PartitionSpec as P

QUERY_HEADS = 64
KEY_VALUE_HEADS = 8
HEAD_WIDTH = 128
GROUP = QUERY_HEADS // KEY_VALUE_HEADS
SCALE = HEAD_WIDTH ** (-0.5)
LOG2E = 1.4426950408889634
TILE = 2 * GROUP
PAIRS = KEY_VALUE_HEADS // 2
LSE_ROWS = 16
QUERY_CHUNKS = 4
OUT_CHUNKS = 4


def kernel(n, home_ref, lengths_ref, q_ref, fresh_ref, prefix_ref, suffix_ref, out_ref,
           obuf, rbuf, lbuf, kbuf, vbuf, skbuf, svbuf,
           load_sem, qsend, qrecv, osend, orecv, *qbufs):
    me = lax.axis_index("blk")
    f32, bf16 = jnp.float32, jnp.bfloat16
    loads = [
        pltpu.make_async_copy(prefix_ref.at[0], kbuf, load_sem.at[0]),
        pltpu.make_async_copy(prefix_ref.at[1], vbuf, load_sem.at[1]),
        pltpu.make_async_copy(suffix_ref.at[0, 0], skbuf, load_sem.at[2]),
        pltpu.make_async_copy(suffix_ref.at[0, 1], svbuf, load_sem.at[3]),
    ]
    for load in loads:
        load.start()

    barrier = pltpu.get_barrier_semaphore()

    def greet(k, _):
        peer = lax.rem(me + k, n)
        pl.semaphore_signal(barrier, inc=1, device_id={"blk": peer},
                            device_id_type=pl.DeviceIdType.MESH)
        return 0

    lax.fori_loop(1, n, greet, 0)

    def find(r, carry):
        row, length = carry
        here = home_ref[r] == me
        return jnp.where(here, r, row), jnp.where(here, lengths_ref[r], length)

    slot_row, slot_len = lax.fori_loop(0, n, find, (jnp.int32(0), jnp.int32(0)))

    pl.semaphore_wait(barrier, n - 1)

    q_rows = QUERY_HEADS // QUERY_CHUNKS

    def q_send(c):
        rows = pl.ds(c * q_rows, q_rows)

        def body(k, _):
            peer = lax.rem(me + k, n)
            pltpu.make_async_remote_copy(
                src_ref=q_ref.at[rows], dst_ref=qbufs[c].at[me],
                send_sem=qsend.at[c], recv_sem=qrecv.at[c],
                device_id={"blk": peer}, device_id_type=pl.DeviceIdType.MESH,
            ).start()
            return 0

        lax.fori_loop(1, n, body, 0)

    for c in range(QUERY_CHUNKS):
        q_send(c)
        qbufs[c][me] = q_ref[pl.ds(c * q_rows, q_rows), :]

    def q_wait(sem, c):
        part = qbufs[c].at[pl.ds(0, n - 1)]
        pltpu.make_async_copy(part, part, sem.at[c]).wait()

    o_rows = QUERY_HEADS // OUT_CHUNKS

    def o_span(c):
        extra = LSE_ROWS if c == OUT_CHUNKS - 1 else 0
        return pl.ds(c * o_rows, o_rows + extra)

    def o_send(c):
        rows = o_span(c)

        def body(k, _):
            peer = lax.rem(me + k, n)
            pltpu.make_async_remote_copy(
                src_ref=obuf.at[peer, rows], dst_ref=rbuf.at[me, rows],
                send_sem=osend.at[c], recv_sem=orecv.at[c],
                device_id={"blk": peer}, device_id_type=pl.DeviceIdType.MESH,
            ).start()
            return 0

        lax.fori_loop(1, n, body, 0)

    def o_wait(sem, c):
        part = rbuf.at[pl.ds(0, n - 1), o_span(c)]
        pltpu.make_async_copy(part, part, sem.at[c]).wait()

    batch = 16 if n % 16 == 0 else n
    live = lax.broadcasted_iota(jnp.int32, (GROUP, skbuf.shape[0]), 1) < slot_len
    lane = lax.broadcasted_iota(jnp.int32, (1, 1, HEAD_WIDTH), 2)
    row_id = lax.broadcasted_iota(jnp.int32, (batch, 1, 1), 0)
    nt = (((1,), (1,)), ((), ()))

    def softmax_part(scores, values):
        peak = jnp.max(scores, axis=-1, keepdims=True)
        p = jnp.exp2((scores - peak) * (SCALE * LOG2E))
        total = jnp.sum(p, axis=-1, keepdims=True)
        acc = jnp.dot(p.astype(bf16), values, preferred_element_type=f32)
        return peak, total, acc

    for pair in range(PAIRS):
        if pair % (PAIRS // QUERY_CHUNKS) == 0:
            q_wait(qrecv, pair // (PAIRS // QUERY_CHUNKS))
        if pair == 0:
            for load in loads:
                load.wait()
        tile = pl.ds(pair * TILE, TILE)
        qbuf = qbufs[pair // (PAIRS // QUERY_CHUNKS)]
        q_tile = pl.ds(pair % (PAIRS // QUERY_CHUNKS) * TILE, TILE)
        slot_q = qbuf[slot_row, q_tile, :].astype(f32)
        suffix = []
        for i in range(2):
            cols = pl.ds((2 * pair + i) * HEAD_WIDTH, HEAD_WIDTH)
            q = slot_q[i * GROUP:(i + 1) * GROUP].astype(bf16)
            s = lax.dot_general(q, skbuf[:, cols], nt, preferred_element_type=f32)
            s = jnp.where(live, s, -jnp.inf)
            suffix.append(softmax_part(s, svbuf[:, cols]))

        def rows_step(b, _, pair=pair, tile=tile, suffix=suffix, qbuf=qbuf, q_tile=q_tile):
            rows = pl.ds(b * batch, batch)
            is_slot = row_id + b * batch == slot_row
            q_all = qbuf[rows, q_tile, :].astype(f32)
            outs = []
            lse_tile = lbuf[rows]
            for i in range(2):
                head = 2 * pair + i
                cols = pl.ds(head * HEAD_WIDTH, HEAD_WIDTH)
                q = q_all[:, i * GROUP:(i + 1) * GROUP, :].reshape(batch * GROUP, HEAD_WIDTH)
                s = lax.dot_general(q.astype(bf16), kbuf[:, cols], nt, preferred_element_type=f32)
                m_p, l_p, a_p = softmax_part(s, vbuf[:, cols])
                m_p = m_p.reshape(batch, GROUP, 1)
                l_p = l_p.reshape(batch, GROUP, 1)
                a_p = a_p.reshape(batch, GROUP, HEAD_WIDTH)
                m_s, l_s, a_s = suffix[i]
                m_s = jnp.where(is_slot, m_s[None], -jnp.inf)
                peak = jnp.maximum(m_p, m_s)
                f_p = jnp.exp2((m_p - peak) * (SCALE * LOG2E))
                f_s = jnp.exp2((m_s - peak) * (SCALE * LOG2E))
                total = f_p * l_p + f_s * l_s[None]
                acc = f_p * a_p + f_s * a_s[None]
                outs.append(acc / total)
                lse = peak * SCALE + jnp.log(total)
                lse_tile = jnp.where(lax.rem(lane, 8) == head, lse, lse_tile)
            obuf[rows, tile, :] = jnp.concatenate(outs, axis=1).astype(bf16)
            if pair < PAIRS - 1:
                lbuf[rows] = lse_tile
            else:
                hi = lse_tile.astype(bf16).astype(f32)
                rest = lse_tile - hi
                mid = rest.astype(bf16).astype(f32)
                parts = [jnp.where(lane < 8, hi, rest - mid), mid]
                obuf[rows, pl.ds(QUERY_HEADS, LSE_ROWS), :] = (
                    jnp.concatenate(parts, axis=1).astype(bf16))
            return 0

        if pair == 0:
            lbuf[...] = jnp.zeros_like(lbuf)
        if n == batch:
            rows_step(0, 0)
        else:
            lax.fori_loop(0, n // batch, rows_step, 0)
        if (pair + 1) % (PAIRS // OUT_CHUNKS) == 0:
            o_send(pair // (PAIRS // OUT_CHUNKS))

    rbuf[me] = obuf[me]

    fresh = fresh_ref[0].astype(f32)
    own_q = q_ref[...].astype(f32)
    new_lse = jnp.zeros((GROUP, HEAD_WIDTH), f32)
    for head in range(KEY_VALUE_HEADS):
        cols = slice(head * HEAD_WIDTH, (head + 1) * HEAD_WIDTH)
        s = jnp.sum(own_q[head * GROUP:(head + 1) * GROUP] * fresh[0:1, cols],
                    axis=-1, keepdims=True) * SCALE
        new_lse = jnp.where(lane[0] == head, s, new_lse)

    for c in range(OUT_CHUNKS):
        o_wait(orecv, c)

    parts = rbuf[:, pl.ds(QUERY_HEADS, LSE_ROWS), :].astype(f32)
    hi = parts[:, :GROUP, :]
    mid = parts[:, GROUP:, :]
    lo = pltpu.roll(hi, HEAD_WIDTH - 8, 2)
    lse = (hi + mid) + lo
    top = jnp.maximum(jnp.max(lse, axis=0), new_lse)
    weights = jnp.exp(lse - top[None])
    new_weight = jnp.exp(new_lse - top)
    inverse = 1.0 / (jnp.sum(weights, axis=0) + new_weight)
    weights = weights * inverse[None]
    new_weight = new_weight * inverse
    for pair in range(PAIRS):
        tile = pl.ds(pair * TILE, TILE)
        blocks = rbuf[:, tile, :].astype(f32)
        outs = []
        for i in range(2):
            head = 2 * pair + i
            cols = slice(head * HEAD_WIDTH, (head + 1) * HEAD_WIDTH)
            part = blocks[:, i * GROUP:(i + 1) * GROUP, :]
            acc = jnp.sum(weights[:, :, head:head + 1] * part, axis=0)
            outs.append(acc + new_weight[:, head:head + 1] * fresh[1:2, cols])
        out_ref[tile, :] = jnp.concatenate(outs, axis=0).astype(bf16)

    for c in range(QUERY_CHUNKS):
        q_wait(qsend, c)
    for c in range(OUT_CHUNKS):
        o_wait(osend, c)


def per_device(queries, prefix_key_value, suffix_key_value, fresh_key_value, lengths, home):
    n = lax.axis_size("blk")
    prefix = prefix_key_value.shape[1]
    slots = suffix_key_value.shape[2]
    width = KEY_VALUE_HEADS * HEAD_WIDTH
    q = queries.reshape(QUERY_HEADS, HEAD_WIDTH)
    bf16 = jnp.bfloat16
    flops = 4 * QUERY_HEADS * HEAD_WIDTH * (n * prefix + slots)
    out = pl.pallas_call(
        functools.partial(kernel, n),
        out_shape=jax.ShapeDtypeStruct((QUERY_HEADS, HEAD_WIDTH), bf16),
        in_specs=[
            pl.BlockSpec(memory_space=pltpu.SMEM),
            pl.BlockSpec(memory_space=pltpu.SMEM),
            pl.BlockSpec(memory_space=pltpu.VMEM),
            pl.BlockSpec(memory_space=pltpu.VMEM),
            pl.BlockSpec(memory_space=pl.ANY),
            pl.BlockSpec(memory_space=pl.ANY),
        ],
        out_specs=pl.BlockSpec(memory_space=pltpu.VMEM),
        scratch_shapes=[
            pltpu.VMEM((n, QUERY_HEADS + LSE_ROWS, HEAD_WIDTH), bf16),
            pltpu.VMEM((n, QUERY_HEADS + LSE_ROWS, HEAD_WIDTH), bf16),
            pltpu.VMEM((n, GROUP, HEAD_WIDTH), jnp.float32),
            pltpu.VMEM((prefix, width), bf16),
            pltpu.VMEM((prefix, width), bf16),
            pltpu.VMEM((slots, width), bf16),
            pltpu.VMEM((slots, width), bf16),
            pltpu.SemaphoreType.DMA((4,)),
            pltpu.SemaphoreType.DMA((QUERY_CHUNKS,)),
            pltpu.SemaphoreType.DMA((QUERY_CHUNKS,)),
            pltpu.SemaphoreType.DMA((OUT_CHUNKS,)),
            pltpu.SemaphoreType.DMA((OUT_CHUNKS,)),
        ] + [
            pltpu.VMEM((n, QUERY_HEADS // QUERY_CHUNKS, HEAD_WIDTH), bf16)
        ] * QUERY_CHUNKS,
        compiler_params=pltpu.CompilerParams(
            collective_id=0, has_side_effects=True, vmem_limit_bytes=48 * 1024 * 1024
        ),
        cost_estimate=pl.CostEstimate(
            flops=flops, bytes_accessed=4 * width * (prefix + slots),
            transcendentals=QUERY_HEADS * n * prefix,
        ),
    )(home, lengths, q, fresh_key_value, prefix_key_value, suffix_key_value)
    return out.reshape(1, QUERY_HEADS * HEAD_WIDTH)


def solution(mesh):
    placed = (
        P(("groups", "blk"), None),
        P(None, ("groups", "blk"), None),
        P(("groups", "blk"), None, None, None),
        P(("groups", "blk"), None, None),
        P("groups"),
        P("groups"),
    )
    return jax.shard_map(
        per_device,
        mesh=mesh,
        in_specs=placed,
        out_specs=P(("groups", "blk"), None),
        check_vma=False,
    )
```

```python
import functools

import jax
import jax.numpy as jnp
from jax import lax
from jax.experimental import pallas as pl
from jax.experimental.pallas import tpu as pltpu
from jax.sharding import PartitionSpec as P

QUERY_HEADS = 64
KEY_VALUE_HEADS = 8
HEAD_WIDTH = 128
GROUP = QUERY_HEADS // KEY_VALUE_HEADS
SCALE = HEAD_WIDTH ** (-0.5)
LOG2E = 1.4426950408889634
TILE = 2 * GROUP
PAIRS = KEY_VALUE_HEADS // 2
LSE_ROWS = 16
CORES = 2
MESH = pl.DeviceIdType.MESH


def kernel(n, home_ref, lengths_ref, q_ref, fresh_ref, prefix_ref, suffix_ref, out_ref,
           home, lengths, q_in, fresh_in, xbuf, sib, obuf, rbuf, lbuf,
           kbuf, vbuf, skbuf, svbuf,
           load_sem, qsend, qrecv, fsend, frecv, ssend, srecv, osend, orecv, *qbufs):
    f32, bf16 = jnp.float32, jnp.bfloat16
    me = lax.axis_index("blk")
    chips = n // CORES
    chip, core = me // CORES, lax.rem(me, CORES)
    sibling = chip * CORES + 1 - core
    my_place = core * chips + chip
    mine = pl.ds(core * chips, chips)
    theirs = pl.ds((1 - core) * chips, chips)

    def peer_of(k):
        return lax.rem(chip + k, chips) * CORES + core

    loads = [
        pltpu.make_async_copy(q_ref, q_in, load_sem.at[0]),
        pltpu.make_async_copy(home_ref, home, load_sem.at[1]),
        pltpu.make_async_copy(lengths_ref, lengths, load_sem.at[2]),
        pltpu.make_async_copy(prefix_ref.at[0], kbuf, load_sem.at[3]),
        pltpu.make_async_copy(suffix_ref.at[0, 0], skbuf, load_sem.at[4]),
        pltpu.make_async_copy(prefix_ref.at[1], vbuf, load_sem.at[5]),
        pltpu.make_async_copy(suffix_ref.at[0, 1], svbuf, load_sem.at[6]),
        pltpu.make_async_copy(fresh_ref, fresh_in, load_sem.at[7]),
    ]
    for load in loads:
        load.start()

    barrier = pltpu.get_barrier_semaphore()
    pl.semaphore_signal(barrier, inc=1, device_id={"blk": sibling}, device_id_type=MESH)

    def greet(k, _):
        pl.semaphore_signal(barrier, inc=1, device_id={"blk": peer_of(k)}, device_id_type=MESH)
        return 0

    lax.fori_loop(1, chips, greet, 0)

    loads[0].wait()
    own_q = q_in[...].astype(f32).reshape(QUERY_HEADS, HEAD_WIDTH)
    for c in range(PAIRS):
        qbufs[c][my_place] = own_q[c * TILE:(c + 1) * TILE].astype(bf16)

    pl.semaphore_wait(barrier, chips)

    for c in range(PAIRS):
        def q_send(k, _, c=c):
            pltpu.make_async_remote_copy(
                src_ref=qbufs[c].at[my_place], dst_ref=qbufs[c].at[my_place],
                send_sem=qsend.at[c], recv_sem=qrecv.at[c],
                device_id={"blk": peer_of(k)}, device_id_type=MESH,
            ).start()
            return 0

        lax.fori_loop(1, chips, q_send, 0)

    def wait_for(part, sem):
        pltpu.make_async_copy(part, part, sem).wait()

    def forward(c):
        return pltpu.make_async_remote_copy(
            src_ref=qbufs[c].at[mine], dst_ref=qbufs[c].at[mine],
            send_sem=fsend.at[c], recv_sem=frecv.at[c],
            device_id={"blk": sibling}, device_id_type=MESH,
        )

    def swap(c):
        return pltpu.make_async_remote_copy(
            src_ref=xbuf.at[c, theirs], dst_ref=sib.at[c],
            send_sem=ssend.at[c], recv_sem=srecv.at[c],
            device_id={"blk": sibling}, device_id_type=MESH,
        )

    def o_span(c):
        return pl.ds(c * TILE, TILE + (LSE_ROWS if c == PAIRS - 1 else 0))

    def o_send(c):
        rows = o_span(c)

        def body(k, _):
            pltpu.make_async_remote_copy(
                src_ref=obuf.at[lax.rem(chip + k, chips), rows], dst_ref=rbuf.at[chip, rows],
                send_sem=osend.at[c], recv_sem=orecv.at[c],
                device_id={"blk": peer_of(k)}, device_id_type=MESH,
            ).start()
            return 0

        lax.fori_loop(1, chips, body, 0)

    loads[1].wait()
    loads[2].wait()

    def find(r, carry):
        row, length = carry
        here = home[r] == me
        return jnp.where(here, r, row), jnp.where(here, lengths[r], length)

    slot_row, slot_len = lax.fori_loop(0, n, find, (jnp.int32(0), jnp.int32(0)))
    slot_place = lax.rem(slot_row, CORES) * chips + slot_row // CORES

    batch = 16 if n % 16 == 0 else n
    live = lax.broadcasted_iota(jnp.int32, (GROUP, skbuf.shape[0]), 1) < slot_len
    lane = lax.broadcasted_iota(jnp.int32, (1, 1, HEAD_WIDTH), 2)
    row_id = lax.broadcasted_iota(jnp.int32, (batch, 1, 1), 0)
    nt = (((1,), (1,)), ((), ()))

    def softmax_part(scores, values):
        peak = jnp.max(scores, axis=-1, keepdims=True)
        p = jnp.exp2((scores - peak) * (SCALE * LOG2E))
        total = jnp.sum(p, axis=-1, keepdims=True)
        acc = jnp.dot(p.astype(bf16), values, preferred_element_type=f32)
        return peak, total, acc

    def merge(c):
        a, b = xbuf[c, mine], sib[c]
        a_lse, b_lse = a[:, TILE:], b[:, TILE:]
        top = jnp.maximum(a_lse, b_lse)
        a_w, b_w = jnp.exp(a_lse - top), jnp.exp(b_lse - top)
        total = a_w + b_w
        obuf[:, pl.ds(c * TILE, TILE), :] = (
            (a_w * a[:, :TILE] + b_w * b[:, :TILE]) / total).astype(bf16)
        lse = top + jnp.log(total)
        tile = lbuf[...]
        for i in range(2):
            tile = jnp.where(lax.rem(lane, 8) == 2 * c + i,
                             lse[:, i * GROUP:(i + 1) * GROUP], tile)
        if c < PAIRS - 1:
            lbuf[...] = tile
        else:
            hi = tile.astype(bf16).astype(f32)
            rest = tile - hi
            mid = rest.astype(bf16).astype(f32)
            parts = [jnp.where(lane < 8, hi, rest - mid), mid]
            obuf[:, pl.ds(QUERY_HEADS, LSE_ROWS), :] = (
                jnp.concatenate(parts, axis=1).astype(bf16))
        o_send(c)

    lbuf[...] = jnp.zeros_like(lbuf)

    def pass_on(c):
        wait_for(qbufs[c].at[pl.ds(0, chips - 1)], qrecv.at[c])
        forward(c).start()

    pass_on(0)
    for pair in range(PAIRS):
        if pair + 1 < PAIRS:
            pass_on(pair + 1)
        forward(pair).wait_recv()
        if pair == 0:
            for load in loads[3:]:
                load.wait()
        qbuf = qbufs[pair]
        slot_q = qbuf[slot_place].astype(f32)
        suffix = []
        for i in range(2):
            cols = pl.ds((2 * pair + i) * HEAD_WIDTH, HEAD_WIDTH)
            q = slot_q[i * GROUP:(i + 1) * GROUP].astype(bf16)
            s = lax.dot_general(q, skbuf[:, cols], nt, preferred_element_type=f32)
            s = jnp.where(live, s, -jnp.inf)
            suffix.append(softmax_part(s, svbuf[:, cols]))

        def rows_step(b, _, pair=pair, suffix=suffix, qbuf=qbuf):
            rows = pl.ds(b * batch, batch)
            is_slot = row_id + b * batch == slot_place
            q_all = qbuf[rows].astype(f32)
            outs, lses = [], []
            for i in range(2):
                cols = pl.ds((2 * pair + i) * HEAD_WIDTH, HEAD_WIDTH)
                q = q_all[:, i * GROUP:(i + 1) * GROUP, :].reshape(batch * GROUP, HEAD_WIDTH)
                s = lax.dot_general(q.astype(bf16), kbuf[:, cols], nt, preferred_element_type=f32)
                m_p, l_p, a_p = softmax_part(s, vbuf[:, cols])
                m_p = m_p.reshape(batch, GROUP, 1)
                l_p = l_p.reshape(batch, GROUP, 1)
                a_p = a_p.reshape(batch, GROUP, HEAD_WIDTH)
                m_s, l_s, a_s = suffix[i]
                m_s = jnp.where(is_slot, m_s[None], -jnp.inf)
                peak = jnp.maximum(m_p, m_s)
                f_p = jnp.exp2((m_p - peak) * (SCALE * LOG2E))
                f_s = jnp.exp2((m_s - peak) * (SCALE * LOG2E))
                total = f_p * l_p + f_s * l_s[None]
                acc = f_p * a_p + f_s * a_s[None]
                outs.append(acc / total)
                lse = peak * SCALE + jnp.log(total)
                lses.append(jnp.broadcast_to(lse, acc.shape))
            xbuf[pair, rows] = jnp.concatenate(outs + lses, axis=1)
            return 0

        if n == batch:
            rows_step(0, 0)
        else:
            lax.fori_loop(0, n // batch, rows_step, 0)
        swap(pair).start()
        if pair > 0:
            swap(pair - 1).wait_recv()
            merge(pair - 1)

    fresh = fresh_in[0].astype(f32)
    new_lse = jnp.zeros((GROUP, HEAD_WIDTH), f32)
    for head in range(KEY_VALUE_HEADS):
        cols = slice(head * HEAD_WIDTH, (head + 1) * HEAD_WIDTH)
        q = qbufs[head // 2][my_place].astype(f32)
        q = q[(head % 2) * GROUP:(head % 2 + 1) * GROUP]
        s = jnp.sum(q * fresh[0:1, cols], axis=-1, keepdims=True) * SCALE
        new_lse = jnp.where(lane[0] == head, s, new_lse)

    swap(PAIRS - 1).wait_recv()
    merge(PAIRS - 1)
    rbuf[chip] = obuf[chip]

    for c in range(PAIRS):
        wait_for(rbuf.at[pl.ds(0, chips - 1), o_span(c)], orecv.at[c])

    parts = rbuf[:, pl.ds(QUERY_HEADS, LSE_ROWS), :].astype(f32)
    hi = parts[:, :GROUP, :]
    mid = parts[:, GROUP:, :]
    lo = pltpu.roll(hi, HEAD_WIDTH - 8, 2)
    lse = (hi + mid) + lo
    top = jnp.maximum(jnp.max(lse, axis=0), new_lse)
    weights = jnp.exp(lse - top[None])
    new_weight = jnp.exp(new_lse - top)
    inverse = 1.0 / (jnp.sum(weights, axis=0) + new_weight)
    weights = weights * inverse[None]
    new_weight = new_weight * inverse
    for pair in range(PAIRS):
        tile = pl.ds(pair * TILE, TILE)
        blocks = rbuf[:, tile, :].astype(f32)
        outs = []
        for i in range(2):
            head = 2 * pair + i
            cols = slice(head * HEAD_WIDTH, (head + 1) * HEAD_WIDTH)
            part = blocks[:, i * GROUP:(i + 1) * GROUP, :]
            acc = jnp.sum(weights[:, :, head:head + 1] * part, axis=0)
            outs.append(acc + new_weight[:, head:head + 1] * fresh[1:2, cols])
        out_ref[tile, :] = jnp.concatenate(outs, axis=0).astype(bf16)

    for c in range(PAIRS):
        wait_for(qbufs[c].at[pl.ds(0, chips - 1)], qsend.at[c])
        forward(c).wait_send()
        swap(c).wait_send()
        wait_for(rbuf.at[pl.ds(0, chips - 1), o_span(c)], osend.at[c])


def per_device(queries, prefix_key_value, suffix_key_value, fresh_key_value, lengths, home):
    n = lax.axis_size("blk")
    chips = n // CORES
    prefix = prefix_key_value.shape[1]
    slots = suffix_key_value.shape[2]
    width = KEY_VALUE_HEADS * HEAD_WIDTH
    f32, bf16 = jnp.float32, jnp.bfloat16
    flops = 4 * QUERY_HEADS * HEAD_WIDTH * (n * prefix + slots)
    dma = pltpu.SemaphoreType.DMA
    out = pl.pallas_call(
        functools.partial(kernel, n),
        out_shape=jax.ShapeDtypeStruct((QUERY_HEADS, HEAD_WIDTH), bf16),
        in_specs=[pl.BlockSpec(memory_space=pl.ANY)] * 6,
        out_specs=pl.BlockSpec(memory_space=pltpu.VMEM),
        scratch_shapes=[
            pltpu.SMEM(home.shape, jnp.int32),
            pltpu.SMEM(lengths.shape, jnp.int32),
            pltpu.VMEM(queries.shape, bf16),
            pltpu.VMEM(fresh_key_value.shape, bf16),
            pltpu.VMEM((PAIRS, n, 2 * TILE, HEAD_WIDTH), f32),
            pltpu.VMEM((PAIRS, chips, 2 * TILE, HEAD_WIDTH), f32),
            pltpu.VMEM((chips, QUERY_HEADS + LSE_ROWS, HEAD_WIDTH), bf16),
            pltpu.VMEM((chips, QUERY_HEADS + LSE_ROWS, HEAD_WIDTH), bf16),
            pltpu.VMEM((chips, GROUP, HEAD_WIDTH), f32),
            pltpu.VMEM((prefix, width), bf16),
            pltpu.VMEM((prefix, width), bf16),
            pltpu.VMEM((slots, width), bf16),
            pltpu.VMEM((slots, width), bf16),
            dma((8,)),
        ] + [dma((PAIRS,))] * 8 + [
            pltpu.VMEM((n, TILE, HEAD_WIDTH), bf16)
        ] * PAIRS,
        compiler_params=pltpu.CompilerParams(
            collective_id=0, has_side_effects=True, vmem_limit_bytes=60 * 1024 * 1024
        ),
        cost_estimate=pl.CostEstimate(
            flops=flops, bytes_accessed=4 * width * (prefix + slots),
            transcendentals=QUERY_HEADS * n * prefix,
        ),
    )(home, lengths, queries, fresh_key_value, prefix_key_value, suffix_key_value)
    return out.reshape(1, QUERY_HEADS * HEAD_WIDTH)


def solution(mesh):
    placed = (
        P(("groups", "blk"), None),
        P(None, ("groups", "blk"), None),
        P(("groups", "blk"), None, None, None),
        P(("groups", "blk"), None, None),
        P("groups"),
        P("groups"),
    )
    return jax.shard_map(
        per_device,
        mesh=mesh,
        in_specs=placed,
        out_specs=P(("groups", "blk"), None),
        check_vma=False,
    )
```

```python
import functools

import jax
import jax.numpy as jnp
from jax import lax
from jax.experimental import pallas as pl
from jax.experimental.pallas import tpu as pltpu
from jax.sharding import PartitionSpec as P

QUERY_HEADS = 64
KEY_VALUE_HEADS = 8
HEAD_WIDTH = 128
GROUP = QUERY_HEADS // KEY_VALUE_HEADS
SCALE = HEAD_WIDTH ** (-0.5)
LOG2E = 1.4426950408889634
TILE = 2 * GROUP
PAIRS = KEY_VALUE_HEADS // 2
CHUNKS = 2
STEP = PAIRS // CHUNKS
ROWS = STEP * TILE
LSE_ROWS = 16
CORES = 2
MESH = pl.DeviceIdType.MESH


def each(first, last, body):
    if last <= 8:
        for k in range(first, last):
            body(k)
    else:
        def step(k, _):
            body(k)
            return 0

        lax.fori_loop(first, last, step, 0)


def kernel(n, home_ref, lengths_ref, q_ref, fresh_ref, prefix_ref, suffix_ref, out_ref,
           home, lengths, q_in, fresh_in, xbuf, sib, obuf, rbuf, lbuf,
           kbuf, vbuf, skbuf, svbuf,
           load_sem, qsend, qrecv, fsend, frecv, ssend, srecv, osend, orecv, *qbufs):
    f32, bf16 = jnp.float32, jnp.bfloat16
    me = lax.axis_index("blk")
    chips = n // CORES
    chip, core = me // CORES, lax.rem(me, CORES)
    sibling = chip * CORES + 1 - core
    my_place = core * chips + chip
    mine = pl.ds(core * chips, chips)
    theirs = pl.ds((1 - core) * chips, chips)

    def peer_of(k):
        return lax.rem(chip + k, chips) * CORES + core

    loads = [
        pltpu.make_async_copy(q_ref, q_in, load_sem.at[0]),
        pltpu.make_async_copy(home_ref, home, load_sem.at[1]),
        pltpu.make_async_copy(lengths_ref, lengths, load_sem.at[2]),
        pltpu.make_async_copy(prefix_ref.at[0], kbuf, load_sem.at[3]),
        pltpu.make_async_copy(suffix_ref.at[0, 0], skbuf, load_sem.at[4]),
        pltpu.make_async_copy(prefix_ref.at[1], vbuf, load_sem.at[5]),
        pltpu.make_async_copy(suffix_ref.at[0, 1], svbuf, load_sem.at[6]),
        pltpu.make_async_copy(fresh_ref, fresh_in, load_sem.at[7]),
    ]
    for load in loads:
        load.start()

    barrier = pltpu.get_barrier_semaphore()
    pl.semaphore_signal(barrier, inc=1, device_id={"blk": sibling}, device_id_type=MESH)

    def greet(k):
        pl.semaphore_signal(barrier, inc=1, device_id={"blk": peer_of(k)}, device_id_type=MESH)

    each(1, chips, greet)

    loads[0].wait()
    own_q = q_in[...].astype(f32).reshape(QUERY_HEADS, HEAD_WIDTH)
    for c in range(CHUNKS):
        qbufs[c][my_place] = own_q[c * ROWS:(c + 1) * ROWS].astype(bf16)

    pl.semaphore_wait(barrier, chips)

    for c in range(CHUNKS):
        def q_send(k, c=c):
            pltpu.make_async_remote_copy(
                src_ref=qbufs[c].at[my_place], dst_ref=qbufs[c].at[my_place],
                send_sem=qsend.at[c], recv_sem=qrecv.at[c],
                device_id={"blk": peer_of(k)}, device_id_type=MESH,
            ).start()

        each(1, chips, q_send)

    def wait_for(part, sem):
        pltpu.make_async_copy(part, part, sem).wait()

    def forward(c):
        return pltpu.make_async_remote_copy(
            src_ref=qbufs[c].at[mine], dst_ref=qbufs[c].at[mine],
            send_sem=fsend.at[c], recv_sem=frecv.at[c],
            device_id={"blk": sibling}, device_id_type=MESH,
        )

    def swap(c):
        return pltpu.make_async_remote_copy(
            src_ref=xbuf.at[c, theirs], dst_ref=sib.at[c],
            send_sem=ssend.at[c], recv_sem=srecv.at[c],
            device_id={"blk": sibling}, device_id_type=MESH,
        )

    def o_span(c):
        return pl.ds(c * ROWS, ROWS + (LSE_ROWS if c == CHUNKS - 1 else 0))

    def o_send(c):
        rows = o_span(c)

        def body(k):
            pltpu.make_async_remote_copy(
                src_ref=obuf.at[lax.rem(chip + k, chips), rows], dst_ref=rbuf.at[chip, rows],
                send_sem=osend.at[c], recv_sem=orecv.at[c],
                device_id={"blk": peer_of(k)}, device_id_type=MESH,
            ).start()

        each(1, chips, body)

    loads[1].wait()
    loads[2].wait()

    def find(r, carry):
        row, length = carry
        here = home[r] == me
        return jnp.where(here, r, row), jnp.where(here, lengths[r], length)

    slot_row, slot_len = lax.fori_loop(0, n, find, (jnp.int32(0), jnp.int32(0)))
    slot_place = lax.rem(slot_row, CORES) * chips + slot_row // CORES

    batch = 16 if n % 16 == 0 else n
    live = lax.broadcasted_iota(jnp.int32, (GROUP, skbuf.shape[0]), 1) < slot_len
    lane = lax.broadcasted_iota(jnp.int32, (1, 1, HEAD_WIDTH), 2)
    row_id = lax.broadcasted_iota(jnp.int32, (batch, 1, 1), 0)
    nt = (((1,), (1,)), ((), ()))

    def softmax_part(scores, values):
        peak = jnp.max(scores, axis=-1, keepdims=True)
        p = jnp.exp2((scores - peak) * (SCALE * LOG2E))
        total = jnp.sum(p, axis=-1, keepdims=True)
        acc = jnp.dot(p.astype(bf16), values, preferred_element_type=f32)
        return peak, total, acc

    def merge(c):
        a, b = xbuf[c, mine], sib[c]
        a_lse, b_lse = a[:, ROWS:], b[:, ROWS:]
        top = jnp.maximum(a_lse, b_lse)
        a_w, b_w = jnp.exp(a_lse - top), jnp.exp(b_lse - top)
        total = a_w + b_w
        obuf[:, pl.ds(c * ROWS, ROWS), :] = (
            (a_w * a[:, :ROWS] + b_w * b[:, :ROWS]) / total).astype(bf16)
        lse = top + jnp.log(total)
        tile = lbuf[...]
        for i in range(2 * STEP):
            tile = jnp.where(lax.rem(lane, 8) == 2 * STEP * c + i,
                             lse[:, i * GROUP:(i + 1) * GROUP], tile)
        if c < CHUNKS - 1:
            lbuf[...] = tile
        else:
            hi = tile.astype(bf16).astype(f32)
            rest = tile - hi
            mid = rest.astype(bf16).astype(f32)
            parts = [jnp.where(lane < 8, hi, rest - mid), mid]
            obuf[:, pl.ds(QUERY_HEADS, LSE_ROWS), :] = (
                jnp.concatenate(parts, axis=1).astype(bf16))
        o_send(c)

    lbuf[...] = jnp.zeros_like(lbuf)

    def pass_on(c):
        wait_for(qbufs[c].at[pl.ds(0, chips - 1)], qrecv.at[c])
        forward(c).start()

    pass_on(0)
    for pair in range(PAIRS):
        chunk, part = pair // STEP, pair % STEP
        if part == 0:
            if chunk + 1 < CHUNKS:
                pass_on(chunk + 1)
            forward(chunk).wait_recv()
        if pair == 0:
            for load in loads[3:]:
                load.wait()
        qbuf = qbufs[chunk]
        tile = pl.ds(part * TILE, TILE)
        slot_q = qbuf[slot_place, tile, :].astype(f32)
        suffix = []
        for i in range(2):
            cols = pl.ds((2 * pair + i) * HEAD_WIDTH, HEAD_WIDTH)
            q = slot_q[i * GROUP:(i + 1) * GROUP].astype(bf16)
            s = lax.dot_general(q, skbuf[:, cols], nt, preferred_element_type=f32)
            s = jnp.where(live, s, -jnp.inf)
            suffix.append(softmax_part(s, svbuf[:, cols]))

        def rows_step(b, _, pair=pair, suffix=suffix, qbuf=qbuf, tile=tile, chunk=chunk, part=part):
            rows = pl.ds(b * batch, batch)
            is_slot = row_id + b * batch == slot_place
            q_all = qbuf[rows, tile, :].astype(f32)
            outs, lses = [], []
            for i in range(2):
                cols = pl.ds((2 * pair + i) * HEAD_WIDTH, HEAD_WIDTH)
                q = q_all[:, i * GROUP:(i + 1) * GROUP, :].reshape(batch * GROUP, HEAD_WIDTH)
                s = lax.dot_general(q.astype(bf16), kbuf[:, cols], nt, preferred_element_type=f32)
                m_p, l_p, a_p = softmax_part(s, vbuf[:, cols])
                m_p = m_p.reshape(batch, GROUP, 1)
                l_p = l_p.reshape(batch, GROUP, 1)
                a_p = a_p.reshape(batch, GROUP, HEAD_WIDTH)
                m_s, l_s, a_s = suffix[i]
                m_s = jnp.where(is_slot, m_s[None], -jnp.inf)
                peak = jnp.maximum(m_p, m_s)
                f_p = jnp.exp2((m_p - peak) * (SCALE * LOG2E))
                f_s = jnp.exp2((m_s - peak) * (SCALE * LOG2E))
                total = f_p * l_p + f_s * l_s[None]
                acc = f_p * a_p + f_s * a_s[None]
                outs.append(acc / total)
                lse = peak * SCALE + jnp.log(total)
                lses.append(jnp.broadcast_to(lse, acc.shape))
            xbuf[chunk, rows, tile, :] = jnp.concatenate(outs, axis=1)
            xbuf[chunk, rows, pl.ds(ROWS + part * TILE, TILE), :] = jnp.concatenate(lses, axis=1)
            return 0

        if n == batch:
            rows_step(0, 0)
        else:
            lax.fori_loop(0, n // batch, rows_step, 0)
        if part == STEP - 1:
            swap(chunk).start()
        if part == 0 and chunk > 0:
            swap(chunk - 1).wait_recv()
            merge(chunk - 1)

    fresh = fresh_in[0].astype(f32)
    new_lse = jnp.zeros((GROUP, HEAD_WIDTH), f32)
    for head in range(KEY_VALUE_HEADS):
        cols = slice(head * HEAD_WIDTH, (head + 1) * HEAD_WIDTH)
        q = own_q[head * GROUP:(head + 1) * GROUP]
        s = jnp.sum(q * fresh[0:1, cols], axis=-1, keepdims=True) * SCALE
        new_lse = jnp.where(lane[0] == head, s, new_lse)

    swap(CHUNKS - 1).wait_recv()
    merge(CHUNKS - 1)
    rbuf[chip] = obuf[chip]

    for c in range(CHUNKS):
        wait_for(rbuf.at[pl.ds(0, chips - 1), o_span(c)], orecv.at[c])

    parts = rbuf[:, pl.ds(QUERY_HEADS, LSE_ROWS), :].astype(f32)
    hi = parts[:, :GROUP, :]
    mid = parts[:, GROUP:, :]
    lo = pltpu.roll(hi, HEAD_WIDTH - 8, 2)
    lse = (hi + mid) + lo
    top = jnp.maximum(jnp.max(lse, axis=0), new_lse)
    weights = jnp.exp(lse - top[None])
    new_weight = jnp.exp(new_lse - top)
    inverse = 1.0 / (jnp.sum(weights, axis=0) + new_weight)
    weights = weights * inverse[None]
    new_weight = new_weight * inverse
    outs = []
    for pair in range(PAIRS):
        tile = pl.ds(pair * TILE, TILE)
        blocks = rbuf[:, tile, :].astype(f32)
        for i in range(2):
            head = 2 * pair + i
            cols = slice(head * HEAD_WIDTH, (head + 1) * HEAD_WIDTH)
            part = blocks[:, i * GROUP:(i + 1) * GROUP, :]
            acc = jnp.sum(weights[:, :, head:head + 1] * part, axis=0)
            outs.append(acc + new_weight[:, head:head + 1] * fresh[1:2, cols])
    out_ref[...] = jnp.concatenate(outs, axis=0).reshape(out_ref.shape).astype(bf16)

    for c in range(CHUNKS):
        wait_for(qbufs[c].at[pl.ds(0, chips - 1)], qsend.at[c])
        forward(c).wait_send()
        swap(c).wait_send()
        wait_for(rbuf.at[pl.ds(0, chips - 1), o_span(c)], osend.at[c])


def per_device(queries, prefix_key_value, suffix_key_value, fresh_key_value, lengths, home):
    n = lax.axis_size("blk")
    chips = n // CORES
    prefix = prefix_key_value.shape[1]
    slots = suffix_key_value.shape[2]
    width = KEY_VALUE_HEADS * HEAD_WIDTH
    f32, bf16 = jnp.float32, jnp.bfloat16
    flops = 4 * QUERY_HEADS * HEAD_WIDTH * (n * prefix + slots)
    dma = pltpu.SemaphoreType.DMA
    out = pl.pallas_call(
        functools.partial(kernel, n),
        out_shape=jax.ShapeDtypeStruct(queries.shape, bf16),
        in_specs=[pl.BlockSpec(memory_space=pl.ANY)] * 6,
        out_specs=pl.BlockSpec(memory_space=pltpu.VMEM),
        scratch_shapes=[
            pltpu.SMEM(home.shape, jnp.int32),
            pltpu.SMEM(lengths.shape, jnp.int32),
            pltpu.VMEM(queries.shape, bf16),
            pltpu.VMEM(fresh_key_value.shape, bf16),
            pltpu.VMEM((CHUNKS, n, 2 * ROWS, HEAD_WIDTH), f32),
            pltpu.VMEM((CHUNKS, chips, 2 * ROWS, HEAD_WIDTH), f32),
            pltpu.VMEM((chips, QUERY_HEADS + LSE_ROWS, HEAD_WIDTH), bf16),
            pltpu.VMEM((chips, QUERY_HEADS + LSE_ROWS, HEAD_WIDTH), bf16),
            pltpu.VMEM((chips, GROUP, HEAD_WIDTH), f32),
            pltpu.VMEM((prefix, width), bf16),
            pltpu.VMEM((prefix, width), bf16),
            pltpu.VMEM((slots, width), bf16),
            pltpu.VMEM((slots, width), bf16),
            dma((8,)),
        ] + [dma((CHUNKS,))] * 8 + [
            pltpu.VMEM((n, ROWS, HEAD_WIDTH), bf16)
        ] * CHUNKS,
        compiler_params=pltpu.CompilerParams(
            collective_id=0, has_side_effects=True, vmem_limit_bytes=60 * 1024 * 1024
        ),
        cost_estimate=pl.CostEstimate(
            flops=flops, bytes_accessed=4 * width * (prefix + slots),
            transcendentals=QUERY_HEADS * n * prefix,
        ),
    )(home, lengths, queries, fresh_key_value, prefix_key_value, suffix_key_value)
    return out


def solution(mesh):
    placed = (
        P(("groups", "blk"), None),
        P(None, ("groups", "blk"), None),
        P(("groups", "blk"), None, None, None),
        P(("groups", "blk"), None, None),
        P("groups"),
        P("groups"),
    )
    return jax.shard_map(
        per_device,
        mesh=mesh,
        in_specs=placed,
        out_specs=P(("groups", "blk"), None),
        check_vma=False,
    )
```

```python
import functools

import jax
import jax.numpy as jnp
from jax import lax
from jax.experimental import pallas as pl
from jax.experimental.pallas import tpu as pltpu
from jax.sharding import PartitionSpec as P

QUERY_HEADS = 64
KEY_VALUE_HEADS = 8
HEAD_WIDTH = 128
GROUP = QUERY_HEADS // KEY_VALUE_HEADS
SCALE = HEAD_WIDTH ** (-0.5)
LOG2E = 1.4426950408889634
TILE = 2 * GROUP
PAIRS = KEY_VALUE_HEADS // 2
BATCH = HEAD_WIDTH // GROUP
STATS = 8
CORES = 2
MESH = pl.DeviceIdType.MESH
NEW_ROWS = 16


def each(first, last, body):
    if last <= 8:
        for k in range(first, last):
            body(k)
    else:
        def step(k, _):
            body(k)
            return 0

        lax.fori_loop(first, last, step, 0)


def kernel(n, prefix, slots, home_ref, lengths_ref, q_ref, fresh_ref, prefix_ref, suffix_ref,
           out_ref, home, lengths, q_in, fresh_in, xbuf, sib, wide, obuf, rbuf, lbuf, rlse,
           kbuf, vbuf, vt,
           load_sem, qsend, qrecv, fsend, frecv, ssend, srecv, osend, orecv, lsend, lrecv,
           *qbufs):
    f32, bf16 = jnp.float32, jnp.bfloat16
    me = lax.axis_index("blk")
    chips = n // CORES
    batches = n // BATCH
    keys = prefix + slots
    chip, core = me // CORES, lax.rem(me, CORES)
    sibling = chip * CORES + 1 - core
    my_place = core * chips + chip
    mine = pl.ds(core * chips, chips)

    def peer_of(k):
        return lax.rem(chip + k, chips) * CORES + core

    loads = [
        pltpu.make_async_copy(q_ref, q_in, load_sem.at[0]),
        pltpu.make_async_copy(home_ref, home, load_sem.at[1]),
        pltpu.make_async_copy(lengths_ref, lengths, load_sem.at[2]),
        pltpu.make_async_copy(fresh_ref, fresh_in, load_sem.at[3]),
        pltpu.make_async_copy(prefix_ref.at[1], vbuf.at[pl.ds(0, prefix)], load_sem.at[4]),
        pltpu.make_async_copy(suffix_ref.at[0, 1], vbuf.at[pl.ds(prefix, slots)], load_sem.at[5]),
        pltpu.make_async_copy(prefix_ref.at[0], kbuf.at[pl.ds(0, prefix)], load_sem.at[6]),
        pltpu.make_async_copy(suffix_ref.at[0, 0], kbuf.at[pl.ds(prefix, slots)], load_sem.at[7]),
    ]
    for load in loads:
        load.start()

    barrier = pltpu.get_barrier_semaphore()
    pl.semaphore_signal(barrier, inc=1, device_id={"blk": sibling}, device_id_type=MESH)

    def greet(k):
        pl.semaphore_signal(barrier, inc=1, device_id={"blk": peer_of(k)}, device_id_type=MESH)

    each(1, chips, greet)

    loads[0].wait()
    own_q = q_in[...].astype(f32).reshape(QUERY_HEADS, HEAD_WIDTH)
    for c in range(PAIRS):
        qbufs[c][my_place] = own_q[c * TILE:(c + 1) * TILE].astype(bf16)

    pl.semaphore_wait(barrier, chips)

    for c in range(PAIRS):
        def q_send(k, c=c):
            pltpu.make_async_remote_copy(
                src_ref=qbufs[c].at[my_place], dst_ref=qbufs[c].at[my_place],
                send_sem=qsend.at[c], recv_sem=qrecv.at[c],
                device_id={"blk": peer_of(k)}, device_id_type=MESH,
            ).start()

        each(1, chips, q_send)

    def wait_for(part, sem):
        pltpu.make_async_copy(part, part, sem).wait()

    def forward(c):
        return pltpu.make_async_remote_copy(
            src_ref=qbufs[c].at[mine], dst_ref=qbufs[c].at[mine],
            send_sem=fsend.at[c], recv_sem=frecv.at[c],
            device_id={"blk": sibling}, device_id_type=MESH,
        )

    def swap(c):
        return pltpu.make_async_remote_copy(
            src_ref=xbuf.at[c], dst_ref=sib.at[c],
            send_sem=ssend.at[c], recv_sem=srecv.at[c],
            device_id={"blk": sibling}, device_id_type=MESH,
        )

    def o_send(c):
        rows = pl.ds(c * TILE, TILE)

        def body(k):
            pltpu.make_async_remote_copy(
                src_ref=obuf.at[lax.rem(chip + k, chips), rows], dst_ref=rbuf.at[chip, rows],
                send_sem=osend.at[c], recv_sem=orecv.at[c],
                device_id={"blk": peer_of(k)}, device_id_type=MESH,
            ).start()

        each(1, chips, body)

    def lse_send(k):
        place = core * chips + lax.rem(chip + k, chips)
        pltpu.make_async_remote_copy(
            src_ref=lbuf.at[place // BATCH], dst_ref=rlse.at[chip],
            send_sem=lsend, recv_sem=lrecv,
            device_id={"blk": peer_of(k)}, device_id_type=MESH,
        ).start()

    loads[1].wait()
    loads[2].wait()

    def find(r, carry):
        row, length = carry
        here = home[r] == me
        return jnp.where(here, r, row), jnp.where(here, lengths[r], length)

    slot_row, slot_len = lax.fori_loop(0, n, find, (jnp.int32(0), jnp.int32(0)))
    slot_place = lax.rem(slot_row, CORES) * chips + slot_row // CORES

    loads[3].wait()
    fresh = fresh_in[0].astype(f32)
    first = lax.broadcasted_iota(jnp.int32, (NEW_ROWS, 1), 0) == 0
    kbuf[pl.ds(keys, NEW_ROWS), :] = jnp.where(first, fresh[0:1], 0.0).astype(bf16)
    new_values = jnp.where(first, fresh[1:2], 0.0).astype(bf16)

    def turn(pair):
        for head in (2 * pair, 2 * pair + 1):
            cols = pl.ds(head * HEAD_WIDTH, HEAD_WIDTH)
            vt[cols, :] = vbuf[:, cols].T

    pair_lane = lax.broadcasted_iota(jnp.int32, (1, 2 * HEAD_WIDTH), 1)
    place_of_lane = lax.rem(pair_lane, HEAD_WIDTH) // GROUP
    slot_id = lax.broadcasted_iota(jnp.int32, (slots, 1), 0)
    stat_id = lax.broadcasted_iota(jnp.int32, (STATS, 1), 0)
    nt = (((1,), (1,)), ((), ()))
    tn = (((0,), (0,)), ((), ()))
    factor = SCALE * LOG2E

    def attend(pair, b):
        q_all = qbufs[pair][pl.ds(b * BATCH, BATCH)].astype(f32)
        q0 = q_all[:, :GROUP, :].reshape(HEAD_WIDTH, HEAD_WIDTH)
        q1 = q_all[:, GROUP:, :].reshape(HEAD_WIDTH, HEAD_WIDTH)
        zero = jnp.zeros_like(q0)
        q = jnp.concatenate([jnp.concatenate([q0, zero], axis=1),
                             jnp.concatenate([zero, q1], axis=1)], axis=0).astype(bf16)
        cols = pl.ds(pair * 2 * HEAD_WIDTH, 2 * HEAD_WIDTH)
        s = lax.dot_general(kbuf[:, cols], q, nt, preferred_element_type=f32)
        place = place_of_lane + b * BATCH
        live = slot_id < jnp.where(place == slot_place, slot_len, 0)
        s_new = jnp.where(first & (place == my_place), s[keys:], -jnp.inf)
        s = jnp.concatenate([s[:prefix], jnp.where(live, s[prefix:keys], -jnp.inf)], axis=0)
        peak = jnp.maximum(jnp.max(s, axis=0, keepdims=True),
                           jnp.max(s_new, axis=0, keepdims=True))
        p = jnp.exp2((s - peak) * factor)
        p_new = jnp.exp2((s_new - peak) * factor)
        total = jnp.sum(p, axis=0, keepdims=True) + jnp.sum(p_new, axis=0, keepdims=True)
        p, p_new = p.astype(bf16), p_new.astype(bf16)
        stats = jnp.zeros((STATS, HEAD_WIDTH), f32)
        for i in range(2):
            head = 2 * pair + i
            lanes = slice(i * HEAD_WIDTH, (i + 1) * HEAD_WIDTH)
            rows = slice(head * HEAD_WIDTH, (head + 1) * HEAD_WIDTH)
            acc = jnp.dot(vt[rows, :], p[:, lanes], preferred_element_type=f32)
            acc += lax.dot_general(new_values[:, rows], p_new[:, lanes], tn,
                                   preferred_element_type=f32)
            xbuf[pair, b, pl.ds(i * HEAD_WIDTH, HEAD_WIDTH), :] = acc
            stats = jnp.where(stat_id == i, peak[:, lanes], stats)
            stats = jnp.where(stat_id == 2 + i, total[:, lanes], stats)
        xbuf[pair, b, pl.ds(2 * HEAD_WIDTH, STATS), :] = stats

    def join(pair, b):
        x_stats = xbuf[pair, b, pl.ds(2 * HEAD_WIDTH, STATS), :]
        y_stats = sib[pair, b, pl.ds(2 * HEAD_WIDTH, STATS), :]
        outs = []
        lses = lbuf[b]
        for i in range(2):
            rows = pl.ds(i * HEAD_WIDTH, HEAD_WIDTH)
            x_m, y_m = x_stats[i:i + 1], y_stats[i:i + 1]
            peak = jnp.maximum(x_m, y_m)
            x_w, y_w = jnp.exp2((x_m - peak) * factor), jnp.exp2((y_m - peak) * factor)
            total = x_w * x_stats[2 + i:3 + i] + y_w * y_stats[2 + i:3 + i]
            inverse = 1.0 / total
            out = xbuf[pair, b, rows, :] * (x_w * inverse) + sib[pair, b, rows, :] * (y_w * inverse)
            outs.append(out.T.reshape(BATCH, GROUP, HEAD_WIDTH))
            lse = peak * SCALE + jnp.log(total)
            lses = jnp.where(stat_id == 2 * pair + i, lse, lses)
        wide[pl.ds(b * BATCH, BATCH)] = jnp.concatenate(outs, axis=1)
        lbuf[b] = lses

    def over_batches(step, pair):
        if batches == 1:
            step(pair, 0)
        else:
            def body(b, _):
                step(pair, b)
                return 0

            lax.fori_loop(0, batches, body, 0)

    def merge(pair):
        swap(pair).wait_recv()
        over_batches(join, pair)
        obuf[:, pl.ds(pair * TILE, TILE), :] = wide[mine].astype(bf16)
        o_send(pair)

    def pass_on(c):
        wait_for(qbufs[c].at[pl.ds(0, chips - 1)], qrecv.at[c])
        forward(c).start()

    lbuf[...] = jnp.zeros_like(lbuf)
    loads[4].wait()
    loads[5].wait()
    turn(0)
    pass_on(0)
    turn(1)
    loads[6].wait()
    loads[7].wait()
    for pair in range(PAIRS):
        if pair + 1 < PAIRS:
            pass_on(pair + 1)
        forward(pair).wait_recv()
        over_batches(attend, pair)
        if pair + 2 < PAIRS:
            turn(pair + 2)
        swap(pair).start()
        if pair > 0:
            merge(pair - 1)
    merge(PAIRS - 1)
    each(1, chips, lse_send)
    rbuf[chip] = obuf[chip]
    rlse[chip] = lbuf[my_place // BATCH]

    wait_for(rlse.at[pl.ds(0, chips - 1)], lrecv)
    lse = rlse[...]
    weights = jnp.exp(lse - jnp.max(lse, axis=0, keepdims=True))
    weights = weights / jnp.sum(weights, axis=0, keepdims=True)
    weights = weights.reshape(chips * KEY_VALUE_HEADS, HEAD_WIDTH)
    shift = lax.rem(HEAD_WIDTH - lax.rem(my_place, BATCH) * GROUP, HEAD_WIDTH)
    weights = pltpu.roll(weights, shift, 1).T[:GROUP]
    outs = []
    for pair in range(PAIRS):
        tile = pl.ds(pair * TILE, TILE)
        wait_for(rbuf.at[pl.ds(0, chips - 1), tile], orecv.at[pair])
        blocks = rbuf[:, tile, :].astype(f32)
        for i in range(2):
            acc = jnp.zeros((GROUP, HEAD_WIDTH), f32)
            for other in range(chips):
                at = other * KEY_VALUE_HEADS + 2 * pair + i
                acc += weights[:, at:at + 1] * blocks[other, i * GROUP:(i + 1) * GROUP, :]
            outs.append(acc)
    out_ref[...] = jnp.concatenate(outs, axis=0).reshape(out_ref.shape).astype(bf16)

    for c in range(PAIRS):
        wait_for(qbufs[c].at[pl.ds(0, chips - 1)], qsend.at[c])
        forward(c).wait_send()
        swap(c).wait_send()
        wait_for(rbuf.at[pl.ds(0, chips - 1), pl.ds(c * TILE, TILE)], osend.at[c])
    wait_for(rlse.at[pl.ds(0, chips - 1)], lsend)


def per_device(queries, prefix_key_value, suffix_key_value, fresh_key_value, lengths, home):
    n = lax.axis_size("blk")
    chips = n // CORES
    prefix = prefix_key_value.shape[1]
    slots = suffix_key_value.shape[2]
    width = KEY_VALUE_HEADS * HEAD_WIDTH
    f32, bf16 = jnp.float32, jnp.bfloat16
    flops = 4 * QUERY_HEADS * HEAD_WIDTH * (n * prefix + slots)
    dma = pltpu.SemaphoreType.DMA
    wide = 2 * HEAD_WIDTH + STATS
    batches = n // BATCH
    out = pl.pallas_call(
        functools.partial(kernel, n, prefix, slots),
        out_shape=jax.ShapeDtypeStruct(queries.shape, bf16),
        in_specs=[pl.BlockSpec(memory_space=pl.ANY)] * 6,
        out_specs=pl.BlockSpec(memory_space=pltpu.VMEM),
        scratch_shapes=[
            pltpu.SMEM(home.shape, jnp.int32),
            pltpu.SMEM(lengths.shape, jnp.int32),
            pltpu.VMEM(queries.shape, bf16),
            pltpu.VMEM(fresh_key_value.shape, bf16),
            pltpu.VMEM((PAIRS, batches, wide, HEAD_WIDTH), f32),
            pltpu.VMEM((PAIRS, batches, wide, HEAD_WIDTH), f32),
            pltpu.VMEM((n, TILE, HEAD_WIDTH), f32),
            pltpu.VMEM((chips, QUERY_HEADS, HEAD_WIDTH), bf16),
            pltpu.VMEM((chips, QUERY_HEADS, HEAD_WIDTH), bf16),
            pltpu.VMEM((batches, KEY_VALUE_HEADS, HEAD_WIDTH), f32),
            pltpu.VMEM((chips, KEY_VALUE_HEADS, HEAD_WIDTH), f32),
            pltpu.VMEM((prefix + slots + NEW_ROWS, width), bf16),
            pltpu.VMEM((prefix + slots, width), bf16),
            pltpu.VMEM((width, prefix + slots), bf16),
            dma((8,)),
        ] + [dma((PAIRS,))] * 8 + [dma, dma] + [
            pltpu.VMEM((n, TILE, HEAD_WIDTH), bf16)
        ] * PAIRS,
        compiler_params=pltpu.CompilerParams(
            collective_id=0, has_side_effects=True, vmem_limit_bytes=60 * 1024 * 1024
        ),
        cost_estimate=pl.CostEstimate(
            flops=flops, bytes_accessed=4 * width * (prefix + slots),
            transcendentals=QUERY_HEADS * n * prefix,
        ),
    )(home, lengths, queries, fresh_key_value, prefix_key_value, suffix_key_value)
    return out


def solution(mesh):
    placed = (
        P(("groups", "blk"), None),
        P(None, ("groups", "blk"), None),
        P(("groups", "blk"), None, None, None),
        P(("groups", "blk"), None, None),
        P("groups"),
        P("groups"),
    )
    return jax.shard_map(
        per_device,
        mesh=mesh,
        in_specs=placed,
        out_specs=P(("groups", "blk"), None),
        check_vma=False,
    )
```

```python
import functools

import jax
import jax.numpy as jnp
from jax import lax
from jax.experimental import pallas as pl
from jax.experimental.pallas import tpu as pltpu
from jax.sharding import PartitionSpec as P

QUERY_HEADS = 64
KEY_VALUE_HEADS = 8
HEAD_WIDTH = 128
GROUP = QUERY_HEADS // KEY_VALUE_HEADS
SCALE = HEAD_WIDTH ** (-0.5)
LOG2E = 1.4426950408889634
TILE = 2 * GROUP
PAIRS = KEY_VALUE_HEADS // 2
BATCH = HEAD_WIDTH // GROUP
STATS = 8
CORES = 2
MESH = pl.DeviceIdType.MESH
NEW_ROWS = 16


def each(first, last, body):
    if last <= 8:
        for k in range(first, last):
            body(k)
    else:
        def step(k, _):
            body(k)
            return 0

        lax.fori_loop(first, last, step, 0)


def kernel(n, prefix, slots, home_ref, lengths_ref, q_ref, fresh_ref, prefix_ref, suffix_ref,
           out_ref, home, lengths, q_in, fresh_in, xbuf, sib, wide, obuf, rbuf, lbuf, rlse,
           kbuf, vbuf, vt,
           load_sem, qsend, qrecv, fsend, frecv, ssend, srecv, osend, orecv, lsend, lrecv,
           *qbufs):
    f32, bf16 = jnp.float32, jnp.bfloat16
    me = lax.axis_index("blk")
    chips = n // CORES
    batches = n // BATCH
    keys = prefix + slots
    chip, core = me // CORES, lax.rem(me, CORES)
    sibling = chip * CORES + 1 - core
    my_place = core * chips + chip
    mine = pl.ds(core * chips, chips)

    def peer_of(k):
        return lax.rem(chip + k, chips) * CORES + core

    loads = [
        pltpu.make_async_copy(q_ref, q_in, load_sem.at[0]),
        pltpu.make_async_copy(home_ref, home, load_sem.at[1]),
        pltpu.make_async_copy(lengths_ref, lengths, load_sem.at[2]),
        pltpu.make_async_copy(fresh_ref, fresh_in, load_sem.at[3]),
        pltpu.make_async_copy(prefix_ref.at[1], vbuf.at[pl.ds(0, prefix)], load_sem.at[4]),
        pltpu.make_async_copy(suffix_ref.at[0, 1], vbuf.at[pl.ds(prefix, slots)], load_sem.at[5]),
        pltpu.make_async_copy(prefix_ref.at[0], kbuf.at[pl.ds(0, prefix)], load_sem.at[6]),
        pltpu.make_async_copy(suffix_ref.at[0, 0], kbuf.at[pl.ds(prefix, slots)], load_sem.at[7]),
    ]
    for load in loads:
        load.start()

    barrier = pltpu.get_barrier_semaphore()
    pl.semaphore_signal(barrier, inc=1, device_id={"blk": sibling}, device_id_type=MESH)

    def greet(k):
        pl.semaphore_signal(barrier, inc=1, device_id={"blk": peer_of(k)}, device_id_type=MESH)

    each(1, chips, greet)

    loads[0].wait()
    own_q = q_in[...].astype(f32).reshape(QUERY_HEADS, HEAD_WIDTH)
    for c in range(PAIRS):
        qbufs[c][my_place] = own_q[c * TILE:(c + 1) * TILE].astype(bf16)

    pl.semaphore_wait(barrier, chips)

    for c in range(PAIRS):
        def q_send(k, c=c):
            pltpu.make_async_remote_copy(
                src_ref=qbufs[c].at[my_place], dst_ref=qbufs[c].at[my_place],
                send_sem=qsend.at[c], recv_sem=qrecv.at[c],
                device_id={"blk": peer_of(k)}, device_id_type=MESH,
            ).start()

        each(1, chips, q_send)

    def wait_for(part, sem):
        pltpu.make_async_copy(part, part, sem).wait()

    def forward(c):
        return pltpu.make_async_remote_copy(
            src_ref=qbufs[c].at[mine], dst_ref=qbufs[c].at[mine],
            send_sem=fsend.at[c], recv_sem=frecv.at[c],
            device_id={"blk": sibling}, device_id_type=MESH,
        )

    def swap(c):
        return pltpu.make_async_remote_copy(
            src_ref=xbuf.at[c], dst_ref=sib.at[c],
            send_sem=ssend.at[c], recv_sem=srecv.at[c],
            device_id={"blk": sibling}, device_id_type=MESH,
        )

    def o_send(c):
        rows = pl.ds(c * TILE, TILE)

        def body(k):
            pltpu.make_async_remote_copy(
                src_ref=obuf.at[lax.rem(chip + k, chips), rows], dst_ref=rbuf.at[chip, rows],
                send_sem=osend.at[c], recv_sem=orecv.at[c],
                device_id={"blk": peer_of(k)}, device_id_type=MESH,
            ).start()

        each(1, chips, body)

    def lse_send(k):
        place = core * chips + lax.rem(chip + k, chips)
        pltpu.make_async_remote_copy(
            src_ref=lbuf.at[place // BATCH], dst_ref=rlse.at[chip],
            send_sem=lsend, recv_sem=lrecv,
            device_id={"blk": peer_of(k)}, device_id_type=MESH,
        ).start()

    loads[1].wait()
    loads[2].wait()

    def find(r, carry):
        row, length = carry
        here = home[r] == me
        return jnp.where(here, r, row), jnp.where(here, lengths[r], length)

    slot_row, slot_len = lax.fori_loop(0, n, find, (jnp.int32(0), jnp.int32(0)))
    slot_place = lax.rem(slot_row, CORES) * chips + slot_row // CORES

    loads[3].wait()
    fresh = fresh_in[0].astype(f32)
    first = lax.broadcasted_iota(jnp.int32, (NEW_ROWS, 1), 0) == 0
    kbuf[pl.ds(keys, NEW_ROWS), :] = jnp.where(first, fresh[0:1], 0.0).astype(bf16)
    new_values = jnp.where(first, fresh[1:2], 0.0).astype(bf16)

    def turn(pair):
        for head in (2 * pair, 2 * pair + 1):
            cols = pl.ds(head * HEAD_WIDTH, HEAD_WIDTH)
            vt[cols, :] = vbuf[:, cols].T

    pair_lane = lax.broadcasted_iota(jnp.int32, (1, 2 * HEAD_WIDTH), 1)
    place_of_lane = lax.rem(pair_lane, HEAD_WIDTH) // GROUP
    slot_id = lax.broadcasted_iota(jnp.int32, (slots, 1), 0)
    stat_id = lax.broadcasted_iota(jnp.int32, (STATS, 1), 0)
    nt = (((1,), (1,)), ((), ()))
    tn = (((0,), (0,)), ((), ()))
    factor = SCALE * LOG2E

    def attend(pair, b):
        q_all = qbufs[pair][pl.ds(b * BATCH, BATCH)].astype(f32)
        q0 = q_all[:, :GROUP, :].reshape(HEAD_WIDTH, HEAD_WIDTH)
        q1 = q_all[:, GROUP:, :].reshape(HEAD_WIDTH, HEAD_WIDTH)
        zero = jnp.zeros_like(q0)
        q = jnp.concatenate([jnp.concatenate([q0, zero], axis=1),
                             jnp.concatenate([zero, q1], axis=1)], axis=0).astype(bf16)
        cols = pl.ds(pair * 2 * HEAD_WIDTH, 2 * HEAD_WIDTH)
        s = lax.dot_general(kbuf[:, cols], q, nt, preferred_element_type=f32)
        place = place_of_lane + b * BATCH
        live = slot_id < jnp.where(place == slot_place, slot_len, 0)
        s_new = jnp.where(first & (place == my_place), s[keys:], -jnp.inf)
        s = jnp.concatenate([s[:prefix], jnp.where(live, s[prefix:keys], -jnp.inf)], axis=0)
        peak = jnp.maximum(jnp.max(s, axis=0, keepdims=True),
                           jnp.max(s_new, axis=0, keepdims=True))
        p = jnp.exp2((s - peak) * factor)
        p_new = jnp.exp2((s_new - peak) * factor)
        total = jnp.sum(p, axis=0, keepdims=True) + jnp.sum(p_new, axis=0, keepdims=True)
        p, p_new = p.astype(bf16), p_new.astype(bf16)
        stats = jnp.zeros((STATS, HEAD_WIDTH), f32)
        for i in range(2):
            head = 2 * pair + i
            lanes = slice(i * HEAD_WIDTH, (i + 1) * HEAD_WIDTH)
            rows = slice(head * HEAD_WIDTH, (head + 1) * HEAD_WIDTH)
            acc = jnp.dot(vt[rows, :], p[:, lanes], preferred_element_type=f32)
            acc += lax.dot_general(new_values[:, rows], p_new[:, lanes], tn,
                                   preferred_element_type=f32)
            xbuf[pair, b, pl.ds(i * HEAD_WIDTH, HEAD_WIDTH), :] = acc
            stats = jnp.where(stat_id == i, peak[:, lanes], stats)
            stats = jnp.where(stat_id == 2 + i, total[:, lanes], stats)
        xbuf[pair, b, pl.ds(2 * HEAD_WIDTH, STATS), :] = stats

    def join(pair, b):
        x_stats = xbuf[pair, b, pl.ds(2 * HEAD_WIDTH, STATS), :]
        y_stats = sib[pair, b, pl.ds(2 * HEAD_WIDTH, STATS), :]
        outs = []
        lses = lbuf[b]
        for i in range(2):
            rows = pl.ds(i * HEAD_WIDTH, HEAD_WIDTH)
            x_m, y_m = x_stats[i:i + 1], y_stats[i:i + 1]
            peak = jnp.maximum(x_m, y_m)
            x_w, y_w = jnp.exp2((x_m - peak) * factor), jnp.exp2((y_m - peak) * factor)
            total = x_w * x_stats[2 + i:3 + i] + y_w * y_stats[2 + i:3 + i]
            inverse = 1.0 / total
            out = xbuf[pair, b, rows, :] * (x_w * inverse) + sib[pair, b, rows, :] * (y_w * inverse)
            outs.append(out.T.reshape(BATCH, GROUP, HEAD_WIDTH))
            lse = peak * SCALE + jnp.log(total)
            lses = jnp.where(stat_id == 2 * pair + i, lse, lses)
        wide[pl.ds(b * BATCH, BATCH)] = jnp.concatenate(outs, axis=1)
        lbuf[b] = lses

    def over_batches(step, pair):
        if batches == 1:
            step(pair, 0)
        else:
            def body(b, _):
                step(pair, b)
                return 0

            lax.fori_loop(0, batches, body, 0)

    def merge(pair):
        swap(pair).wait_recv()
        over_batches(join, pair)
        obuf[:, pl.ds(pair * TILE, TILE), :] = wide[mine].astype(bf16)
        o_send(pair)

    def pass_on(c):
        wait_for(qbufs[c].at[pl.ds(0, chips - 1)], qrecv.at[c])
        forward(c).start()

    lbuf[...] = jnp.zeros_like(lbuf)
    loads[4].wait()
    loads[5].wait()
    for pair in range(PAIRS):
        turn(pair)
    pass_on(0)
    loads[6].wait()
    loads[7].wait()
    for pair in range(PAIRS):
        if pair + 1 < PAIRS:
            pass_on(pair + 1)
        forward(pair).wait_recv()
        over_batches(attend, pair)
        swap(pair).start()
        if pair > 0:
            merge(pair - 1)
    merge(PAIRS - 1)
    each(1, chips, lse_send)
    rbuf[chip] = obuf[chip]
    rlse[chip] = lbuf[my_place // BATCH]

    wait_for(rlse.at[pl.ds(0, chips - 1)], lrecv)
    lse = rlse[...]
    weights = jnp.exp(lse - jnp.max(lse, axis=0, keepdims=True))
    weights = weights / jnp.sum(weights, axis=0, keepdims=True)
    weights = weights.reshape(chips * KEY_VALUE_HEADS, HEAD_WIDTH)
    shift = lax.rem(HEAD_WIDTH - lax.rem(my_place, BATCH) * GROUP, HEAD_WIDTH)
    weights = pltpu.roll(weights, shift, 1).T[:GROUP]
    outs = []
    for pair in range(PAIRS):
        tile = pl.ds(pair * TILE, TILE)
        wait_for(rbuf.at[pl.ds(0, chips - 1), tile], orecv.at[pair])
        blocks = rbuf[:, tile, :].astype(f32)
        for i in range(2):
            acc = jnp.zeros((GROUP, HEAD_WIDTH), f32)
            for other in range(chips):
                at = other * KEY_VALUE_HEADS + 2 * pair + i
                acc += weights[:, at:at + 1] * blocks[other, i * GROUP:(i + 1) * GROUP, :]
            outs.append(acc)
    out_ref[...] = jnp.concatenate(outs, axis=0).reshape(out_ref.shape).astype(bf16)

    for c in range(PAIRS):
        wait_for(qbufs[c].at[pl.ds(0, chips - 1)], qsend.at[c])
        forward(c).wait_send()
        swap(c).wait_send()
        wait_for(rbuf.at[pl.ds(0, chips - 1), pl.ds(c * TILE, TILE)], osend.at[c])
    wait_for(rlse.at[pl.ds(0, chips - 1)], lsend)


def per_device(queries, prefix_key_value, suffix_key_value, fresh_key_value, lengths, home):
    n = lax.axis_size("blk")
    chips = n // CORES
    prefix = prefix_key_value.shape[1]
    slots = suffix_key_value.shape[2]
    width = KEY_VALUE_HEADS * HEAD_WIDTH
    f32, bf16 = jnp.float32, jnp.bfloat16
    flops = 4 * QUERY_HEADS * HEAD_WIDTH * (n * prefix + slots)
    dma = pltpu.SemaphoreType.DMA
    wide = 2 * HEAD_WIDTH + STATS
    batches = n // BATCH
    out = pl.pallas_call(
        functools.partial(kernel, n, prefix, slots),
        out_shape=jax.ShapeDtypeStruct(queries.shape, bf16),
        in_specs=[pl.BlockSpec(memory_space=pl.ANY)] * 6,
        out_specs=pl.BlockSpec(memory_space=pltpu.VMEM),
        scratch_shapes=[
            pltpu.SMEM(home.shape, jnp.int32),
            pltpu.SMEM(lengths.shape, jnp.int32),
            pltpu.VMEM(queries.shape, bf16),
            pltpu.VMEM(fresh_key_value.shape, bf16),
            pltpu.VMEM((PAIRS, batches, wide, HEAD_WIDTH), f32),
            pltpu.VMEM((PAIRS, batches, wide, HEAD_WIDTH), f32),
            pltpu.VMEM((n, TILE, HEAD_WIDTH), f32),
            pltpu.VMEM((chips, QUERY_HEADS, HEAD_WIDTH), bf16),
            pltpu.VMEM((chips, QUERY_HEADS, HEAD_WIDTH), bf16),
            pltpu.VMEM((batches, KEY_VALUE_HEADS, HEAD_WIDTH), f32),
            pltpu.VMEM((chips, KEY_VALUE_HEADS, HEAD_WIDTH), f32),
            pltpu.VMEM((prefix + slots + NEW_ROWS, width), bf16),
            pltpu.VMEM((prefix + slots, width), bf16),
            pltpu.VMEM((width, prefix + slots), bf16),
            dma((8,)),
        ] + [dma((PAIRS,))] * 8 + [dma, dma] + [
            pltpu.VMEM((n, TILE, HEAD_WIDTH), bf16)
        ] * PAIRS,
        compiler_params=pltpu.CompilerParams(
            collective_id=0, has_side_effects=True, vmem_limit_bytes=60 * 1024 * 1024
        ),
        cost_estimate=pl.CostEstimate(
            flops=flops, bytes_accessed=4 * width * (prefix + slots),
            transcendentals=QUERY_HEADS * n * prefix,
        ),
    )(home, lengths, queries, fresh_key_value, prefix_key_value, suffix_key_value)
    return out


def solution(mesh):
    placed = (
        P(("groups", "blk"), None),
        P(None, ("groups", "blk"), None),
        P(("groups", "blk"), None, None, None),
        P(("groups", "blk"), None, None),
        P("groups"),
        P("groups"),
    )
    return jax.shard_map(
        per_device,
        mesh=mesh,
        in_specs=placed,
        out_specs=P(("groups", "blk"), None),
        check_vma=False,
    )
```

```python
import functools

import jax
import jax.numpy as jnp
from jax import lax
from jax.experimental import pallas as pl
from jax.experimental.pallas import tpu as pltpu
from jax.sharding import PartitionSpec as P

QUERY_HEADS = 64
KEY_VALUE_HEADS = 8
HEAD_WIDTH = 128
GROUP = QUERY_HEADS // KEY_VALUE_HEADS
SCALE = HEAD_WIDTH ** (-0.5)
LOG2E = 1.4426950408889634
TILE = 2 * GROUP
PAIRS = KEY_VALUE_HEADS // 2
BATCH = HEAD_WIDTH // GROUP
MESH = pl.DeviceIdType.MESH
NEW_ROWS = 16


def each(first, last, body):
    if last <= 16:
        for k in range(first, last):
            body(k)
    else:
        def step(k, _):
            body(k)
            return 0

        lax.fori_loop(first, last, step, 0)


def kernel(n, prefix, slots, home_ref, lengths_ref, q_ref, fresh_ref, prefix_ref, suffix_ref,
           out_ref, home, lengths, q_in, fresh_in, obuf, rbuf, lbuf, rlse,
           kbuf, vbuf, vt,
           load_sem, qsend, qrecv, osend, orecv, lsend, lrecv,
           *qbufs):
    f32, bf16 = jnp.float32, jnp.bfloat16
    me = lax.axis_index("blk")
    batches = n // BATCH
    keys = prefix + slots

    def peer_of(k):
        return k + jnp.where(k >= me, 1, 0)

    loads = [
        pltpu.make_async_copy(q_ref, q_in, load_sem.at[0]),
        pltpu.make_async_copy(home_ref, home, load_sem.at[1]),
        pltpu.make_async_copy(lengths_ref, lengths, load_sem.at[2]),
        pltpu.make_async_copy(fresh_ref, fresh_in, load_sem.at[3]),
        pltpu.make_async_copy(prefix_ref.at[1], vbuf.at[pl.ds(0, prefix)], load_sem.at[4]),
        pltpu.make_async_copy(suffix_ref.at[0, 1], vbuf.at[pl.ds(prefix, slots)], load_sem.at[5]),
        pltpu.make_async_copy(prefix_ref.at[0], kbuf.at[pl.ds(0, prefix)], load_sem.at[6]),
        pltpu.make_async_copy(suffix_ref.at[0, 0], kbuf.at[pl.ds(prefix, slots)], load_sem.at[7]),
    ]
    for load in loads:
        load.start()

    barrier = pltpu.get_barrier_semaphore()
    def greet(k):
        pl.semaphore_signal(barrier, inc=1, device_id={"blk": peer_of(k)}, device_id_type=MESH)

    each(0, n - 1, greet)

    loads[0].wait()
    own_q = q_in[...].astype(f32).reshape(QUERY_HEADS, HEAD_WIDTH)
    for c in range(PAIRS):
        qbufs[c][me] = own_q[c * TILE:(c + 1) * TILE].astype(bf16)

    pl.semaphore_wait(barrier, n - 1)

    for c in range(PAIRS):
        def q_send(k, c=c):
            k = n - 2 - k
            pltpu.make_async_remote_copy(
                src_ref=qbufs[c].at[me], dst_ref=qbufs[c].at[me],
                send_sem=qsend.at[c], recv_sem=qrecv.at[c],
                device_id={"blk": peer_of(k)}, device_id_type=MESH,
            ).start()

        each(0, n - 1, q_send)

    def wait_for(part, sem):
        pltpu.make_async_copy(part, part, sem).wait()

    def o_send(c):
        rows = pl.ds(c * TILE, TILE)

        def body(k):
            pltpu.make_async_remote_copy(
                src_ref=obuf.at[peer_of(k), rows], dst_ref=rbuf.at[me, rows],
                send_sem=osend.at[c], recv_sem=orecv.at[c],
                device_id={"blk": peer_of(k)}, device_id_type=MESH,
            ).start()

        each(0, n - 1, body)

    def lse_send(k):
        pltpu.make_async_remote_copy(
            src_ref=lbuf.at[peer_of(k) // BATCH], dst_ref=rlse.at[me],
            send_sem=lsend, recv_sem=lrecv,
            device_id={"blk": peer_of(k)}, device_id_type=MESH,
        ).start()

    loads[1].wait()
    loads[2].wait()

    def find(r, carry):
        row, length = carry
        here = home[r] == me
        return jnp.where(here, r, row), jnp.where(here, lengths[r], length)

    slot_row, slot_len = lax.fori_loop(0, n, find, (jnp.int32(0), jnp.int32(0)))

    loads[3].wait()
    fresh = fresh_in[0].astype(f32)
    first = lax.broadcasted_iota(jnp.int32, (NEW_ROWS, 1), 0) == 0
    kbuf[pl.ds(keys, NEW_ROWS), :] = jnp.where(first, fresh[0:1], 0.0).astype(bf16)
    new_values = jnp.where(first, fresh[1:2], 0.0).astype(bf16)

    def turn(pair):
        for head in (2 * pair, 2 * pair + 1):
            cols = pl.ds(head * HEAD_WIDTH, HEAD_WIDTH)
            vt[cols, :] = vbuf[:, cols].T

    pair_lane = lax.broadcasted_iota(jnp.int32, (1, 2 * HEAD_WIDTH), 1)
    place_of_lane = lax.rem(pair_lane, HEAD_WIDTH) // GROUP
    slot_id = lax.broadcasted_iota(jnp.int32, (slots, 1), 0)
    head_id = lax.broadcasted_iota(jnp.int32, (KEY_VALUE_HEADS, 1), 0)
    nt = (((1,), (1,)), ((), ()))
    tn = (((0,), (0,)), ((), ()))
    factor = SCALE * LOG2E

    def attend(pair, b):
        q_all = qbufs[pair][pl.ds(b * BATCH, BATCH)].astype(f32)
        q0 = q_all[:, :GROUP, :].reshape(HEAD_WIDTH, HEAD_WIDTH)
        q1 = q_all[:, GROUP:, :].reshape(HEAD_WIDTH, HEAD_WIDTH)
        zero = jnp.zeros_like(q0)
        q = jnp.concatenate([jnp.concatenate([q0, zero], axis=1),
                             jnp.concatenate([zero, q1], axis=1)], axis=0).astype(bf16)
        cols = pl.ds(pair * 2 * HEAD_WIDTH, 2 * HEAD_WIDTH)
        s = lax.dot_general(kbuf[:, cols], q, nt, preferred_element_type=f32)
        place = place_of_lane + b * BATCH
        live = slot_id < jnp.where(place == slot_row, slot_len, 0)
        s_new = jnp.where(first & (place == me), s[keys:], -jnp.inf)
        s = jnp.concatenate([s[:prefix], jnp.where(live, s[prefix:keys], -jnp.inf)], axis=0)
        peak = jnp.maximum(jnp.max(s, axis=0, keepdims=True),
                           jnp.max(s_new, axis=0, keepdims=True))
        p = jnp.exp2((s - peak) * factor)
        p_new = jnp.exp2((s_new - peak) * factor)
        total = jnp.sum(p, axis=0, keepdims=True) + jnp.sum(p_new, axis=0, keepdims=True)
        p, p_new = p.astype(bf16), p_new.astype(bf16)
        inverse = 1.0 / total
        lse = peak * SCALE + jnp.log(total)
        outs = []
        lses = lbuf[b]
        for i in range(2):
            head = 2 * pair + i
            lanes = slice(i * HEAD_WIDTH, (i + 1) * HEAD_WIDTH)
            rows = slice(head * HEAD_WIDTH, (head + 1) * HEAD_WIDTH)
            acc = jnp.dot(vt[rows, :], p[:, lanes], preferred_element_type=f32)
            acc += lax.dot_general(new_values[:, rows], p_new[:, lanes], tn,
                                   preferred_element_type=f32)
            out = acc * inverse[:, lanes]
            outs.append(out.T.reshape(BATCH, GROUP, HEAD_WIDTH))
            lses = jnp.where(head_id == head, lse[:, lanes], lses)
        tile = pl.ds(pair * TILE, TILE)
        obuf[pl.ds(b * BATCH, BATCH), tile, :] = jnp.concatenate(outs, axis=1).astype(bf16)
        lbuf[b] = lses

    def over_batches(step, pair):
        if batches == 1:
            step(pair, 0)
        else:
            def body(b, _):
                step(pair, b)
                return 0

            lax.fori_loop(0, batches, body, 0)

    lbuf[...] = jnp.zeros_like(lbuf)
    loads[4].wait()
    loads[5].wait()
    for pair in range(PAIRS):
        turn(pair)
    loads[6].wait()
    loads[7].wait()
    for pair in range(PAIRS):
        wait_for(qbufs[pair].at[pl.ds(0, n - 1)], qrecv.at[pair])
        over_batches(attend, pair)
        o_send(pair)
    each(0, n - 1, lse_send)
    rbuf[me] = obuf[me]
    rlse[me] = lbuf[me // BATCH]

    wait_for(rlse.at[pl.ds(0, n - 1)], lrecv)
    lse = rlse[...]
    weights = jnp.exp(lse - jnp.max(lse, axis=0, keepdims=True))
    weights = weights / jnp.sum(weights, axis=0, keepdims=True)
    weights = weights.reshape(n * KEY_VALUE_HEADS, HEAD_WIDTH)
    shift = lax.rem(HEAD_WIDTH - lax.rem(me, BATCH) * GROUP, HEAD_WIDTH)
    weights = pltpu.roll(weights, shift, 1).T[:GROUP]
    outs = []
    for pair in range(PAIRS):
        tile = pl.ds(pair * TILE, TILE)
        wait_for(rbuf.at[pl.ds(0, n - 1), tile], orecv.at[pair])
        blocks = rbuf[:, tile, :].astype(f32)
        for i in range(2):
            acc = jnp.zeros((GROUP, HEAD_WIDTH), f32)
            for other in range(n):
                at = other * KEY_VALUE_HEADS + 2 * pair + i
                acc += weights[:, at:at + 1] * blocks[other, i * GROUP:(i + 1) * GROUP, :]
            outs.append(acc)
    out_ref[...] = jnp.concatenate(outs, axis=0).reshape(out_ref.shape).astype(bf16)

    for c in range(PAIRS):
        wait_for(qbufs[c].at[pl.ds(0, n - 1)], qsend.at[c])
        wait_for(rbuf.at[pl.ds(0, n - 1), pl.ds(c * TILE, TILE)], osend.at[c])
    wait_for(rlse.at[pl.ds(0, n - 1)], lsend)


def per_device(queries, prefix_key_value, suffix_key_value, fresh_key_value, lengths, home):
    n = lax.axis_size("blk")
    prefix = prefix_key_value.shape[1]
    slots = suffix_key_value.shape[2]
    width = KEY_VALUE_HEADS * HEAD_WIDTH
    f32, bf16 = jnp.float32, jnp.bfloat16
    flops = 4 * QUERY_HEADS * HEAD_WIDTH * (n * prefix + slots)
    dma = pltpu.SemaphoreType.DMA
    batches = n // BATCH
    out = pl.pallas_call(
        functools.partial(kernel, n, prefix, slots),
        out_shape=jax.ShapeDtypeStruct(queries.shape, bf16),
        in_specs=[pl.BlockSpec(memory_space=pl.ANY)] * 6,
        out_specs=pl.BlockSpec(memory_space=pltpu.VMEM),
        scratch_shapes=[
            pltpu.SMEM(home.shape, jnp.int32),
            pltpu.SMEM(lengths.shape, jnp.int32),
            pltpu.VMEM(queries.shape, bf16),
            pltpu.VMEM(fresh_key_value.shape, bf16),
            pltpu.VMEM((n, QUERY_HEADS, HEAD_WIDTH), bf16),
            pltpu.VMEM((n, QUERY_HEADS, HEAD_WIDTH), bf16),
            pltpu.VMEM((batches, KEY_VALUE_HEADS, HEAD_WIDTH), f32),
            pltpu.VMEM((n, KEY_VALUE_HEADS, HEAD_WIDTH), f32),
            pltpu.VMEM((prefix + slots + NEW_ROWS, width), bf16),
            pltpu.VMEM((prefix + slots, width), bf16),
            pltpu.VMEM((width, prefix + slots), bf16),
            dma((8,)),
        ] + [dma((PAIRS,))] * 4 + [dma, dma] + [
            pltpu.VMEM((n, TILE, HEAD_WIDTH), bf16)
        ] * PAIRS,
        compiler_params=pltpu.CompilerParams(
            collective_id=0, has_side_effects=True, vmem_limit_bytes=60 * 1024 * 1024
        ),
        cost_estimate=pl.CostEstimate(
            flops=flops, bytes_accessed=4 * width * (prefix + slots),
            transcendentals=QUERY_HEADS * n * prefix,
        ),
    )(home, lengths, queries, fresh_key_value, prefix_key_value, suffix_key_value)
    return out


def solution(mesh):
    placed = (
        P(("groups", "blk"), None),
        P(None, ("groups", "blk"), None),
        P(("groups", "blk"), None, None, None),
        P(("groups", "blk"), None, None),
        P("groups"),
        P("groups"),
    )
    return jax.shard_map(
        per_device,
        mesh=mesh,
        in_specs=placed,
        out_specs=P(("groups", "blk"), None),
        check_vma=False,
    )
```

```python
import functools

import jax
import jax.numpy as jnp
from jax import lax
from jax.experimental import pallas as pl
from jax.experimental.pallas import tpu as pltpu
from jax.sharding import PartitionSpec as P

QUERY_HEADS = 64
KEY_VALUE_HEADS = 8
HEAD_WIDTH = 128
GROUP = QUERY_HEADS // KEY_VALUE_HEADS
SCALE = HEAD_WIDTH ** (-0.5)
LOG2E = 1.4426950408889634
TILE = 2 * GROUP
PAIRS = KEY_VALUE_HEADS // 2
LSE_ROWS = 16
QUERY_CHUNKS = 4
OUT_CHUNKS = 4
MESH = pl.DeviceIdType.MESH


def each(last, body):
    if last <= 16:
        for k in range(last):
            body(k)
    else:
        def step(k, _):
            body(k)
            return 0

        lax.fori_loop(0, last, step, 0)


def kernel(n, home_ref, lengths_ref, q_ref, fresh_ref, prefix_ref, suffix_ref, out_ref,
           home, lengths, q_in, fresh_in, obuf, rbuf, lbuf, kbuf, vbuf, skbuf, svbuf,
           load_sem, qsend, qrecv, osend, orecv, *qbufs):
    me = lax.axis_index("blk")
    f32, bf16 = jnp.float32, jnp.bfloat16

    def peer_of(k):
        return k + jnp.where(k >= me, 1, 0)

    loads = [
        pltpu.make_async_copy(q_ref, q_in, load_sem.at[0]),
        pltpu.make_async_copy(home_ref, home, load_sem.at[1]),
        pltpu.make_async_copy(lengths_ref, lengths, load_sem.at[2]),
        pltpu.make_async_copy(prefix_ref.at[0], kbuf, load_sem.at[3]),
        pltpu.make_async_copy(suffix_ref.at[0, 0], skbuf, load_sem.at[4]),
        pltpu.make_async_copy(prefix_ref.at[1], vbuf, load_sem.at[5]),
        pltpu.make_async_copy(suffix_ref.at[0, 1], svbuf, load_sem.at[6]),
        pltpu.make_async_copy(fresh_ref, fresh_in, load_sem.at[7]),
    ]

    barrier = pltpu.get_barrier_semaphore()

    def greet(k):
        pl.semaphore_signal(barrier, inc=1, device_id={"blk": peer_of(k)}, device_id_type=MESH)

    loads[0].start()
    each(n - 1, greet)
    for load in loads[1:]:
        load.start()

    q_rows = QUERY_HEADS // QUERY_CHUNKS
    loads[0].wait()
    own_q = q_in[...].astype(f32).reshape(QUERY_HEADS, HEAD_WIDTH)
    for c in range(QUERY_CHUNKS):
        qbufs[c][me] = own_q[c * q_rows:(c + 1) * q_rows].astype(bf16)

    pl.semaphore_wait(barrier, n - 1)

    for c in range(QUERY_CHUNKS):
        def q_send(k, c=c):
            pltpu.make_async_remote_copy(
                src_ref=qbufs[c].at[me], dst_ref=qbufs[c].at[me],
                send_sem=qsend.at[c], recv_sem=qrecv.at[c],
                device_id={"blk": peer_of(n - 2 - k)}, device_id_type=MESH,
            ).start()

        each(n - 1, q_send)

    loads[1].wait()
    loads[2].wait()

    def find(r, carry):
        row, length = carry
        here = home[r] == me
        return jnp.where(here, r, row), jnp.where(here, lengths[r], length)

    slot_row, slot_len = lax.fori_loop(0, n, find, (jnp.int32(0), jnp.int32(0)))

    def q_wait(sem, c):
        part = qbufs[c].at[pl.ds(0, n - 1)]
        pltpu.make_async_copy(part, part, sem.at[c]).wait()

    o_rows = QUERY_HEADS // OUT_CHUNKS

    def o_span(c):
        extra = LSE_ROWS if c == OUT_CHUNKS - 1 else 0
        return pl.ds(c * o_rows, o_rows + extra)

    def o_send(c):
        rows = o_span(c)

        def body(k):
            peer = peer_of(k)
            pltpu.make_async_remote_copy(
                src_ref=obuf.at[peer, rows], dst_ref=rbuf.at[me, rows],
                send_sem=osend.at[c], recv_sem=orecv.at[c],
                device_id={"blk": peer}, device_id_type=MESH,
            ).start()

        each(n - 1, body)

    def o_wait(sem, c):
        part = rbuf.at[pl.ds(0, n - 1), o_span(c)]
        pltpu.make_async_copy(part, part, sem.at[c]).wait()

    batch = 16 if n % 16 == 0 else n
    live = lax.broadcasted_iota(jnp.int32, (GROUP, skbuf.shape[0]), 1) < slot_len
    lane = lax.broadcasted_iota(jnp.int32, (1, 1, HEAD_WIDTH), 2)
    row_id = lax.broadcasted_iota(jnp.int32, (batch, 1, 1), 0)
    nt = (((1,), (1,)), ((), ()))

    def softmax_part(scores, values):
        peak = jnp.max(scores, axis=-1, keepdims=True)
        p = jnp.exp2((scores - peak) * (SCALE * LOG2E))
        total = jnp.sum(p, axis=-1, keepdims=True)
        acc = jnp.dot(p.astype(bf16), values, preferred_element_type=f32)
        return peak, total, acc

    for pair in range(PAIRS):
        if pair % (PAIRS // QUERY_CHUNKS) == 0:
            q_wait(qrecv, pair // (PAIRS // QUERY_CHUNKS))
        if pair == 0:
            for load in loads[3:]:
                load.wait()
        tile = pl.ds(pair * TILE, TILE)
        qbuf = qbufs[pair // (PAIRS // QUERY_CHUNKS)]
        q_tile = pl.ds(pair % (PAIRS // QUERY_CHUNKS) * TILE, TILE)
        slot_q = qbuf[slot_row, q_tile, :].astype(f32)
        suffix = []
        for i in range(2):
            cols = pl.ds((2 * pair + i) * HEAD_WIDTH, HEAD_WIDTH)
            q = slot_q[i * GROUP:(i + 1) * GROUP].astype(bf16)
            s = lax.dot_general(q, skbuf[:, cols], nt, preferred_element_type=f32)
            s = jnp.where(live, s, -jnp.inf)
            suffix.append(softmax_part(s, svbuf[:, cols]))

        def rows_step(b, _, pair=pair, tile=tile, suffix=suffix, qbuf=qbuf, q_tile=q_tile):
            rows = pl.ds(b * batch, batch)
            is_slot = row_id + b * batch == slot_row
            q_all = qbuf[rows, q_tile, :].astype(f32)
            outs = []
            lse_tile = lbuf[rows]
            for i in range(2):
                head = 2 * pair + i
                cols = pl.ds(head * HEAD_WIDTH, HEAD_WIDTH)
                q = q_all[:, i * GROUP:(i + 1) * GROUP, :].reshape(batch * GROUP, HEAD_WIDTH)
                s = lax.dot_general(q.astype(bf16), kbuf[:, cols], nt, preferred_element_type=f32)
                m_p, l_p, a_p = softmax_part(s, vbuf[:, cols])
                m_p = m_p.reshape(batch, GROUP, 1)
                l_p = l_p.reshape(batch, GROUP, 1)
                a_p = a_p.reshape(batch, GROUP, HEAD_WIDTH)
                m_s, l_s, a_s = suffix[i]
                m_s = jnp.where(is_slot, m_s[None], -jnp.inf)
                peak = jnp.maximum(m_p, m_s)
                f_p = jnp.exp2((m_p - peak) * (SCALE * LOG2E))
                f_s = jnp.exp2((m_s - peak) * (SCALE * LOG2E))
                total = f_p * l_p + f_s * l_s[None]
                acc = f_p * a_p + f_s * a_s[None]
                outs.append(acc / total)
                lse = peak * SCALE + jnp.log(total)
                lse_tile = jnp.where(lax.rem(lane, 8) == head, lse, lse_tile)
            obuf[rows, tile, :] = jnp.concatenate(outs, axis=1).astype(bf16)
            if pair < PAIRS - 1:
                lbuf[rows] = lse_tile
            else:
                hi = lse_tile.astype(bf16).astype(f32)
                rest = lse_tile - hi
                mid = rest.astype(bf16).astype(f32)
                parts = [jnp.where(lane < 8, hi, rest - mid), mid]
                obuf[rows, pl.ds(QUERY_HEADS, LSE_ROWS), :] = (
                    jnp.concatenate(parts, axis=1).astype(bf16))
            return 0

        if pair == 0:
            lbuf[...] = jnp.zeros_like(lbuf)
        if n == batch:
            rows_step(0, 0)
        else:
            lax.fori_loop(0, n // batch, rows_step, 0)
        if (pair + 1) % (PAIRS // OUT_CHUNKS) == 0:
            o_send(pair // (PAIRS // OUT_CHUNKS))

    rbuf[me] = obuf[me]

    fresh = fresh_in[0].astype(f32)
    new_lse = jnp.zeros((GROUP, HEAD_WIDTH), f32)
    for head in range(KEY_VALUE_HEADS):
        cols = slice(head * HEAD_WIDTH, (head + 1) * HEAD_WIDTH)
        s = jnp.sum(own_q[head * GROUP:(head + 1) * GROUP] * fresh[0:1, cols],
                    axis=-1, keepdims=True) * SCALE
        new_lse = jnp.where(lane[0] == head, s, new_lse)

    for c in range(OUT_CHUNKS):
        o_wait(orecv, c)

    parts = rbuf[:, pl.ds(QUERY_HEADS, LSE_ROWS), :].astype(f32)
    hi = parts[:, :GROUP, :]
    mid = parts[:, GROUP:, :]
    lo = pltpu.roll(hi, HEAD_WIDTH - 8, 2)
    lse = (hi + mid) + lo
    top = jnp.maximum(jnp.max(lse, axis=0), new_lse)
    weights = jnp.exp(lse - top[None])
    new_weight = jnp.exp(new_lse - top)
    inverse = 1.0 / (jnp.sum(weights, axis=0) + new_weight)
    weights = weights * inverse[None]
    new_weight = new_weight * inverse
    outs = []
    for pair in range(PAIRS):
        tile = pl.ds(pair * TILE, TILE)
        blocks = rbuf[:, tile, :].astype(f32)
        for i in range(2):
            head = 2 * pair + i
            cols = slice(head * HEAD_WIDTH, (head + 1) * HEAD_WIDTH)
            part = blocks[:, i * GROUP:(i + 1) * GROUP, :]
            acc = jnp.sum(weights[:, :, head:head + 1] * part, axis=0)
            outs.append(acc + new_weight[:, head:head + 1] * fresh[1:2, cols])
    out_ref[...] = jnp.concatenate(outs, axis=0).reshape(out_ref.shape).astype(bf16)

    for c in range(QUERY_CHUNKS):
        q_wait(qsend, c)
    for c in range(OUT_CHUNKS):
        o_wait(osend, c)


def per_device(queries, prefix_key_value, suffix_key_value, fresh_key_value, lengths, home):
    n = lax.axis_size("blk")
    prefix = prefix_key_value.shape[1]
    slots = suffix_key_value.shape[2]
    width = KEY_VALUE_HEADS * HEAD_WIDTH
    bf16 = jnp.bfloat16
    flops = 4 * QUERY_HEADS * HEAD_WIDTH * (n * prefix + slots)
    out = pl.pallas_call(
        functools.partial(kernel, n),
        out_shape=jax.ShapeDtypeStruct(queries.shape, bf16),
        in_specs=[pl.BlockSpec(memory_space=pl.ANY)] * 6,
        out_specs=pl.BlockSpec(memory_space=pltpu.VMEM),
        scratch_shapes=[
            pltpu.SMEM(home.shape, jnp.int32),
            pltpu.SMEM(lengths.shape, jnp.int32),
            pltpu.VMEM(queries.shape, bf16),
            pltpu.VMEM(fresh_key_value.shape, bf16),
            pltpu.VMEM((n, QUERY_HEADS + LSE_ROWS, HEAD_WIDTH), bf16),
            pltpu.VMEM((n, QUERY_HEADS + LSE_ROWS, HEAD_WIDTH), bf16),
            pltpu.VMEM((n, GROUP, HEAD_WIDTH), jnp.float32),
            pltpu.VMEM((prefix, width), bf16),
            pltpu.VMEM((prefix, width), bf16),
            pltpu.VMEM((slots, width), bf16),
            pltpu.VMEM((slots, width), bf16),
            pltpu.SemaphoreType.DMA((8,)),
            pltpu.SemaphoreType.DMA((QUERY_CHUNKS,)),
            pltpu.SemaphoreType.DMA((QUERY_CHUNKS,)),
            pltpu.SemaphoreType.DMA((OUT_CHUNKS,)),
            pltpu.SemaphoreType.DMA((OUT_CHUNKS,)),
        ] + [
            pltpu.VMEM((n, QUERY_HEADS // QUERY_CHUNKS, HEAD_WIDTH), bf16)
        ] * QUERY_CHUNKS,
        compiler_params=pltpu.CompilerParams(
            collective_id=0, has_side_effects=True, vmem_limit_bytes=60 * 1024 * 1024
        ),
        cost_estimate=pl.CostEstimate(
            flops=flops, bytes_accessed=4 * width * (prefix + slots),
            transcendentals=QUERY_HEADS * n * prefix,
        ),
    )(home, lengths, queries, fresh_key_value, prefix_key_value, suffix_key_value)
    return out


def solution(mesh):
    placed = (
        P(("groups", "blk"), None),
        P(None, ("groups", "blk"), None),
        P(("groups", "blk"), None, None, None),
        P(("groups", "blk"), None, None),
        P("groups"),
        P("groups"),
    )
    return jax.shard_map(
        per_device,
        mesh=mesh,
        in_specs=placed,
        out_specs=P(("groups", "blk"), None),
        check_vma=False,
    )
```

```python
import functools

import jax
import jax.numpy as jnp
from jax import lax
from jax.experimental import pallas as pl
from jax.experimental.pallas import tpu as pltpu
from jax.sharding import PartitionSpec as P

QUERY_HEADS = 64
KEY_VALUE_HEADS = 8
HEAD_WIDTH = 128
GROUP = QUERY_HEADS // KEY_VALUE_HEADS
SCALE = HEAD_WIDTH ** (-0.5)
LOG2E = 1.4426950408889634
TILE = 2 * GROUP
PAIRS = KEY_VALUE_HEADS // 2
LSE_ROWS = 16
QUERY_CHUNKS = 4
OUT_ENDS = (2, 3, 4)
OUT_CHUNKS = len(OUT_ENDS)
MESH = pl.DeviceIdType.MESH


def each(last, body):
    if last <= 16:
        for k in range(last):
            body(k)
    else:
        def step(k, _):
            body(k)
            return 0

        lax.fori_loop(0, last, step, 0)


def kernel(n, home_ref, lengths_ref, q_ref, fresh_ref, prefix_ref, suffix_ref, out_ref,
           home, lengths, q_in, fresh_in, obuf, rbuf, lbuf, kbuf, vbuf, skbuf, svbuf,
           load_sem, qsend, qrecv, osend, orecv, *qbufs):
    me = lax.axis_index("blk")
    f32, bf16 = jnp.float32, jnp.bfloat16

    def peer_of(k):
        return k + jnp.where(k >= me, 1, 0)

    loads = [
        pltpu.make_async_copy(q_ref, q_in, load_sem.at[0]),
        pltpu.make_async_copy(home_ref, home, load_sem.at[1]),
        pltpu.make_async_copy(lengths_ref, lengths, load_sem.at[2]),
        pltpu.make_async_copy(prefix_ref.at[0], kbuf, load_sem.at[3]),
        pltpu.make_async_copy(suffix_ref.at[0, 0], skbuf, load_sem.at[4]),
        pltpu.make_async_copy(prefix_ref.at[1], vbuf, load_sem.at[5]),
        pltpu.make_async_copy(suffix_ref.at[0, 1], svbuf, load_sem.at[6]),
        pltpu.make_async_copy(fresh_ref, fresh_in, load_sem.at[7]),
    ]

    barrier = pltpu.get_barrier_semaphore()

    def greet(k):
        pl.semaphore_signal(barrier, inc=1, device_id={"blk": peer_of(k)}, device_id_type=MESH)

    loads[0].start()
    each(n - 1, greet)
    for load in loads[1:]:
        load.start()

    q_rows = QUERY_HEADS // QUERY_CHUNKS
    loads[0].wait()
    own_q = q_in[...].astype(f32).reshape(QUERY_HEADS, HEAD_WIDTH)
    for c in range(QUERY_CHUNKS):
        qbufs[c][me] = own_q[c * q_rows:(c + 1) * q_rows].astype(bf16)

    pl.semaphore_wait(barrier, n - 1)

    for c in range(QUERY_CHUNKS):
        def q_send(k, c=c):
            pltpu.make_async_remote_copy(
                src_ref=qbufs[c].at[me], dst_ref=qbufs[c].at[me],
                send_sem=qsend.at[c], recv_sem=qrecv.at[c],
                device_id={"blk": peer_of(n - 2 - k)}, device_id_type=MESH,
            ).start()

        each(n - 1, q_send)

    loads[1].wait()
    loads[2].wait()

    def find(r, carry):
        row, length = carry
        here = home[r] == me
        return jnp.where(here, r, row), jnp.where(here, lengths[r], length)

    slot_row, slot_len = lax.fori_loop(0, n, find, (jnp.int32(0), jnp.int32(0)))

    def q_wait(sem, c):
        part = qbufs[c].at[pl.ds(0, n - 1)]
        pltpu.make_async_copy(part, part, sem.at[c]).wait()

    def o_span(c):
        start = OUT_ENDS[c - 1] * TILE if c else 0
        extra = LSE_ROWS if c == OUT_CHUNKS - 1 else 0
        return pl.ds(start, OUT_ENDS[c] * TILE - start + extra)

    def o_send(c):
        rows = o_span(c)

        def body(k):
            peer = peer_of(k)
            pltpu.make_async_remote_copy(
                src_ref=obuf.at[peer, rows], dst_ref=rbuf.at[me, rows],
                send_sem=osend.at[c], recv_sem=orecv.at[c],
                device_id={"blk": peer}, device_id_type=MESH,
            ).start()

        each(n - 1, body)

    def o_wait(sem, c):
        part = rbuf.at[pl.ds(0, n - 1), o_span(c)]
        pltpu.make_async_copy(part, part, sem.at[c]).wait()

    batch = 16 if n % 16 == 0 else n
    live = lax.broadcasted_iota(jnp.int32, (GROUP, skbuf.shape[0]), 1) < slot_len
    lane = lax.broadcasted_iota(jnp.int32, (1, 1, HEAD_WIDTH), 2)
    row_id = lax.broadcasted_iota(jnp.int32, (batch, 1, 1), 0)
    nt = (((1,), (1,)), ((), ()))

    def softmax_part(scores, values):
        peak = jnp.max(scores, axis=-1, keepdims=True)
        p = jnp.exp2((scores - peak) * (SCALE * LOG2E))
        total = jnp.sum(p, axis=-1, keepdims=True)
        acc = jnp.dot(p.astype(bf16), values, preferred_element_type=f32)
        return peak, total, acc

    for pair in range(PAIRS):
        if pair % (PAIRS // QUERY_CHUNKS) == 0:
            q_wait(qrecv, pair // (PAIRS // QUERY_CHUNKS))
        if pair == 0:
            for load in loads[3:]:
                load.wait()
        tile = pl.ds(pair * TILE, TILE)
        qbuf = qbufs[pair // (PAIRS // QUERY_CHUNKS)]
        q_tile = pl.ds(pair % (PAIRS // QUERY_CHUNKS) * TILE, TILE)
        slot_q = qbuf[slot_row, q_tile, :].astype(f32)
        suffix = []
        for i in range(2):
            cols = pl.ds((2 * pair + i) * HEAD_WIDTH, HEAD_WIDTH)
            q = slot_q[i * GROUP:(i + 1) * GROUP].astype(bf16)
            s = lax.dot_general(q, skbuf[:, cols], nt, preferred_element_type=f32)
            s = jnp.where(live, s, -jnp.inf)
            suffix.append(softmax_part(s, svbuf[:, cols]))

        def rows_step(b, _, pair=pair, tile=tile, suffix=suffix, qbuf=qbuf, q_tile=q_tile):
            rows = pl.ds(b * batch, batch)
            is_slot = row_id + b * batch == slot_row
            q_all = qbuf[rows, q_tile, :].astype(f32)
            outs = []
            lse_tile = lbuf[rows]
            for i in range(2):
                head = 2 * pair + i
                cols = pl.ds(head * HEAD_WIDTH, HEAD_WIDTH)
                q = q_all[:, i * GROUP:(i + 1) * GROUP, :].reshape(batch * GROUP, HEAD_WIDTH)
                s = lax.dot_general(q.astype(bf16), kbuf[:, cols], nt, preferred_element_type=f32)
                m_p, l_p, a_p = softmax_part(s, vbuf[:, cols])
                m_p = m_p.reshape(batch, GROUP, 1)
                l_p = l_p.reshape(batch, GROUP, 1)
                a_p = a_p.reshape(batch, GROUP, HEAD_WIDTH)
                m_s, l_s, a_s = suffix[i]
                m_s = jnp.where(is_slot, m_s[None], -jnp.inf)
                peak = jnp.maximum(m_p, m_s)
                f_p = jnp.exp2((m_p - peak) * (SCALE * LOG2E))
                f_s = jnp.exp2((m_s - peak) * (SCALE * LOG2E))
                total = f_p * l_p + f_s * l_s[None]
                acc = f_p * a_p + f_s * a_s[None]
                outs.append(acc / total)
                lse = peak * SCALE + jnp.log(total)
                lse_tile = jnp.where(lax.rem(lane, 8) == head, lse, lse_tile)
            obuf[rows, tile, :] = jnp.concatenate(outs, axis=1).astype(bf16)
            if pair < PAIRS - 1:
                lbuf[rows] = lse_tile
            else:
                hi = lse_tile.astype(bf16).astype(f32)
                rest = lse_tile - hi
                mid = rest.astype(bf16).astype(f32)
                parts = [jnp.where(lane < 8, hi, rest - mid), mid]
                obuf[rows, pl.ds(QUERY_HEADS, LSE_ROWS), :] = (
                    jnp.concatenate(parts, axis=1).astype(bf16))
            return 0

        if pair == 0:
            lbuf[...] = jnp.zeros_like(lbuf)
        if n == batch:
            rows_step(0, 0)
        else:
            lax.fori_loop(0, n // batch, rows_step, 0)
        if pair + 1 in OUT_ENDS:
            o_send(OUT_ENDS.index(pair + 1))

    rbuf[me] = obuf[me]

    fresh = fresh_in[0].astype(f32)
    new_lse = jnp.zeros((GROUP, HEAD_WIDTH), f32)
    for head in range(KEY_VALUE_HEADS):
        cols = slice(head * HEAD_WIDTH, (head + 1) * HEAD_WIDTH)
        s = jnp.sum(own_q[head * GROUP:(head + 1) * GROUP] * fresh[0:1, cols],
                    axis=-1, keepdims=True) * SCALE
        new_lse = jnp.where(lane[0] == head, s, new_lse)

    for c in range(OUT_CHUNKS):
        o_wait(orecv, c)

    parts = rbuf[:, pl.ds(QUERY_HEADS, LSE_ROWS), :].astype(f32)
    hi = parts[:, :GROUP, :]
    mid = parts[:, GROUP:, :]
    lo = pltpu.roll(hi, HEAD_WIDTH - 8, 2)
    lse = (hi + mid) + lo
    top = jnp.maximum(jnp.max(lse, axis=0), new_lse)
    weights = jnp.exp(lse - top[None])
    new_weight = jnp.exp(new_lse - top)
    inverse = 1.0 / (jnp.sum(weights, axis=0) + new_weight)
    weights = weights * inverse[None]
    new_weight = new_weight * inverse
    outs = []
    for pair in range(PAIRS):
        tile = pl.ds(pair * TILE, TILE)
        blocks = rbuf[:, tile, :].astype(f32)
        for i in range(2):
            head = 2 * pair + i
            cols = slice(head * HEAD_WIDTH, (head + 1) * HEAD_WIDTH)
            part = blocks[:, i * GROUP:(i + 1) * GROUP, :]
            acc = jnp.sum(weights[:, :, head:head + 1] * part, axis=0)
            outs.append(acc + new_weight[:, head:head + 1] * fresh[1:2, cols])
    out_ref[...] = jnp.concatenate(outs, axis=0).reshape(out_ref.shape).astype(bf16)

    for c in range(QUERY_CHUNKS):
        q_wait(qsend, c)
    for c in range(OUT_CHUNKS):
        o_wait(osend, c)


def per_device(queries, prefix_key_value, suffix_key_value, fresh_key_value, lengths, home):
    n = lax.axis_size("blk")
    prefix = prefix_key_value.shape[1]
    slots = suffix_key_value.shape[2]
    width = KEY_VALUE_HEADS * HEAD_WIDTH
    bf16 = jnp.bfloat16
    flops = 4 * QUERY_HEADS * HEAD_WIDTH * (n * prefix + slots)
    out = pl.pallas_call(
        functools.partial(kernel, n),
        out_shape=jax.ShapeDtypeStruct(queries.shape, bf16),
        in_specs=[pl.BlockSpec(memory_space=pl.ANY)] * 6,
        out_specs=pl.BlockSpec(memory_space=pltpu.VMEM),
        scratch_shapes=[
            pltpu.SMEM(home.shape, jnp.int32),
            pltpu.SMEM(lengths.shape, jnp.int32),
            pltpu.VMEM(queries.shape, bf16),
            pltpu.VMEM(fresh_key_value.shape, bf16),
            pltpu.VMEM((n, QUERY_HEADS + LSE_ROWS, HEAD_WIDTH), bf16),
            pltpu.VMEM((n, QUERY_HEADS + LSE_ROWS, HEAD_WIDTH), bf16),
            pltpu.VMEM((n, GROUP, HEAD_WIDTH), jnp.float32),
            pltpu.VMEM((prefix, width), bf16),
            pltpu.VMEM((prefix, width), bf16),
            pltpu.VMEM((slots, width), bf16),
            pltpu.VMEM((slots, width), bf16),
            pltpu.SemaphoreType.DMA((8,)),
            pltpu.SemaphoreType.DMA((QUERY_CHUNKS,)),
            pltpu.SemaphoreType.DMA((QUERY_CHUNKS,)),
            pltpu.SemaphoreType.DMA((OUT_CHUNKS,)),
            pltpu.SemaphoreType.DMA((OUT_CHUNKS,)),
        ] + [
            pltpu.VMEM((n, QUERY_HEADS // QUERY_CHUNKS, HEAD_WIDTH), bf16)
        ] * QUERY_CHUNKS,
        compiler_params=pltpu.CompilerParams(
            collective_id=0, has_side_effects=True, vmem_limit_bytes=60 * 1024 * 1024
        ),
        cost_estimate=pl.CostEstimate(
            flops=flops, bytes_accessed=4 * width * (prefix + slots),
            transcendentals=QUERY_HEADS * n * prefix,
        ),
    )(home, lengths, queries, fresh_key_value, prefix_key_value, suffix_key_value)
    return out


def solution(mesh):
    placed = (
        P(("groups", "blk"), None),
        P(None, ("groups", "blk"), None),
        P(("groups", "blk"), None, None, None),
        P(("groups", "blk"), None, None),
        P("groups"),
        P("groups"),
    )
    return jax.shard_map(
        per_device,
        mesh=mesh,
        in_specs=placed,
        out_specs=P(("groups", "blk"), None),
        check_vma=False,
    )
```

```python
import functools

import jax
import jax.numpy as jnp
from jax import lax
from jax.experimental import pallas as pl
from jax.experimental.pallas import tpu as pltpu
from jax.sharding import PartitionSpec as P

QUERY_HEADS = 64
KEY_VALUE_HEADS = 8
HEAD_WIDTH = 128
GROUP = QUERY_HEADS // KEY_VALUE_HEADS
SCALE = HEAD_WIDTH ** (-0.5)
LOG2E = 1.4426950408889634
TILE = 2 * GROUP
PAIRS = KEY_VALUE_HEADS // 2
LSE_ROWS = 16
QUERY_CHUNKS = 4
OUT_CHUNKS = 4
CORES = 2
DIRECT = 2
MESH = pl.DeviceIdType.MESH


def each(last, body):
    if last <= 16:
        for k in range(last):
            body(k)
    else:
        def step(k, _):
            body(k)
            return 0

        lax.fori_loop(0, last, step, 0)


def kernel(n, home_ref, lengths_ref, q_ref, fresh_ref, prefix_ref, suffix_ref, out_ref,
           home, lengths, q_in, fresh_in, obuf, rbuf, lbuf, kbuf, vbuf, skbuf, svbuf,
           load_sem, qsend, qrecv, fsend, frecv, osend, orecv, *qbufs):
    me = lax.axis_index("blk")
    f32, bf16 = jnp.float32, jnp.bfloat16

    def peer_of(k):
        return k + jnp.where(k >= me, 1, 0)

    chips = n // CORES
    chip, core = me // CORES, lax.rem(me, CORES)
    sibling = chip * CORES + 1 - core

    def place_of(block):
        return lax.rem(block, CORES) * chips + block // CORES

    my_place = place_of(me)
    mine = pl.ds(core * chips, chips)

    def forward(c):
        return pltpu.make_async_remote_copy(
            src_ref=qbufs[c].at[mine], dst_ref=qbufs[c].at[mine],
            send_sem=fsend.at[c], recv_sem=frecv.at[c],
            device_id={"blk": sibling}, device_id_type=MESH,
        )

    loads = [
        pltpu.make_async_copy(q_ref, q_in, load_sem.at[0]),
        pltpu.make_async_copy(home_ref, home, load_sem.at[1]),
        pltpu.make_async_copy(lengths_ref, lengths, load_sem.at[2]),
        pltpu.make_async_copy(prefix_ref.at[0], kbuf, load_sem.at[3]),
        pltpu.make_async_copy(suffix_ref.at[0, 0], skbuf, load_sem.at[4]),
        pltpu.make_async_copy(prefix_ref.at[1], vbuf, load_sem.at[5]),
        pltpu.make_async_copy(suffix_ref.at[0, 1], svbuf, load_sem.at[6]),
        pltpu.make_async_copy(fresh_ref, fresh_in, load_sem.at[7]),
    ]

    barrier = pltpu.get_barrier_semaphore()

    def greet(k):
        pl.semaphore_signal(barrier, inc=1, device_id={"blk": peer_of(k)}, device_id_type=MESH)

    loads[0].start()
    each(n - 1, greet)
    for load in loads[1:]:
        load.start()

    q_rows = QUERY_HEADS // QUERY_CHUNKS
    loads[0].wait()
    own_q = q_in[...].astype(f32).reshape(QUERY_HEADS, HEAD_WIDTH)
    for c in range(QUERY_CHUNKS):
        qbufs[c][my_place] = own_q[c * q_rows:(c + 1) * q_rows].astype(bf16)

    pl.semaphore_wait(barrier, n - 1)

    for c in range(QUERY_CHUNKS):
        def q_send(k, c=c):
            if c < DIRECT:
                peer = peer_of(n - 2 - k)
            else:
                other = chips - 2 - k
                peer = (other + jnp.where(other >= chip, 1, 0)) * CORES + core
            pltpu.make_async_remote_copy(
                src_ref=qbufs[c].at[my_place], dst_ref=qbufs[c].at[my_place],
                send_sem=qsend.at[c], recv_sem=qrecv.at[c],
                device_id={"blk": peer}, device_id_type=MESH,
            ).start()

        each(n - 1 if c < DIRECT else chips - 1, q_send)

    loads[1].wait()
    loads[2].wait()

    def find(r, carry):
        row, length = carry
        here = home[r] == me
        return jnp.where(here, r, row), jnp.where(here, lengths[r], length)

    slot_block, slot_len = lax.fori_loop(0, n, find, (jnp.int32(0), jnp.int32(0)))
    slot_row = place_of(slot_block)

    def q_wait(sem, c):
        part = qbufs[c].at[pl.ds(0, n - 1 if c < DIRECT else chips - 1)]
        pltpu.make_async_copy(part, part, sem.at[c]).wait()

    o_rows = QUERY_HEADS // OUT_CHUNKS

    def o_span(c):
        extra = LSE_ROWS if c == OUT_CHUNKS - 1 else 0
        return pl.ds(c * o_rows, o_rows + extra)

    def o_send(c):
        rows = o_span(c)

        def body(k):
            peer = peer_of(k)
            pltpu.make_async_remote_copy(
                src_ref=obuf.at[place_of(peer), rows], dst_ref=rbuf.at[me, rows],
                send_sem=osend.at[c], recv_sem=orecv.at[c],
                device_id={"blk": peer}, device_id_type=MESH,
            ).start()

        each(n - 1, body)

    def o_wait(sem, c):
        part = rbuf.at[pl.ds(0, n - 1), o_span(c)]
        pltpu.make_async_copy(part, part, sem.at[c]).wait()

    batch = 16 if n % 16 == 0 else n
    live = lax.broadcasted_iota(jnp.int32, (GROUP, skbuf.shape[0]), 1) < slot_len
    lane = lax.broadcasted_iota(jnp.int32, (1, 1, HEAD_WIDTH), 2)
    row_id = lax.broadcasted_iota(jnp.int32, (batch, 1, 1), 0)
    nt = (((1,), (1,)), ((), ()))

    def softmax_part(scores, values):
        peak = jnp.max(scores, axis=-1, keepdims=True)
        p = jnp.exp2((scores - peak) * (SCALE * LOG2E))
        total = jnp.sum(p, axis=-1, keepdims=True)
        acc = jnp.dot(p.astype(bf16), values, preferred_element_type=f32)
        return peak, total, acc

    for pair in range(PAIRS):
        if pair % (PAIRS // QUERY_CHUNKS) == 0:
            c = pair // (PAIRS // QUERY_CHUNKS)
            if c < DIRECT:
                q_wait(qrecv, c)
            else:
                forward(c).wait_recv()
            if c > 0 and DIRECT <= c + 1 < QUERY_CHUNKS:
                q_wait(qrecv, c + 1)
                forward(c + 1).start()
        if pair == 0:
            for load in loads[3:]:
                load.wait()
        tile = pl.ds(pair * TILE, TILE)
        qbuf = qbufs[pair // (PAIRS // QUERY_CHUNKS)]
        q_tile = pl.ds(pair % (PAIRS // QUERY_CHUNKS) * TILE, TILE)
        slot_q = qbuf[slot_row, q_tile, :].astype(f32)
        suffix = []
        for i in range(2):
            cols = pl.ds((2 * pair + i) * HEAD_WIDTH, HEAD_WIDTH)
            q = slot_q[i * GROUP:(i + 1) * GROUP].astype(bf16)
            s = lax.dot_general(q, skbuf[:, cols], nt, preferred_element_type=f32)
            s = jnp.where(live, s, -jnp.inf)
            suffix.append(softmax_part(s, svbuf[:, cols]))

        def rows_step(b, _, pair=pair, tile=tile, suffix=suffix, qbuf=qbuf, q_tile=q_tile):
            rows = pl.ds(b * batch, batch)
            is_slot = row_id + b * batch == slot_row
            q_all = qbuf[rows, q_tile, :].astype(f32)
            outs = []
            lse_tile = lbuf[rows]
            for i in range(2):
                head = 2 * pair + i
                cols = pl.ds(head * HEAD_WIDTH, HEAD_WIDTH)
                q = q_all[:, i * GROUP:(i + 1) * GROUP, :].reshape(batch * GROUP, HEAD_WIDTH)
                s = lax.dot_general(q.astype(bf16), kbuf[:, cols], nt, preferred_element_type=f32)
                m_p, l_p, a_p = softmax_part(s, vbuf[:, cols])
                m_p = m_p.reshape(batch, GROUP, 1)
                l_p = l_p.reshape(batch, GROUP, 1)
                a_p = a_p.reshape(batch, GROUP, HEAD_WIDTH)
                m_s, l_s, a_s = suffix[i]
                m_s = jnp.where(is_slot, m_s[None], -jnp.inf)
                peak = jnp.maximum(m_p, m_s)
                f_p = jnp.exp2((m_p - peak) * (SCALE * LOG2E))
                f_s = jnp.exp2((m_s - peak) * (SCALE * LOG2E))
                total = f_p * l_p + f_s * l_s[None]
                acc = f_p * a_p + f_s * a_s[None]
                outs.append(acc / total)
                lse = peak * SCALE + jnp.log(total)
                lse_tile = jnp.where(lax.rem(lane, 8) == head, lse, lse_tile)
            obuf[rows, tile, :] = jnp.concatenate(outs, axis=1).astype(bf16)
            if pair < PAIRS - 1:
                lbuf[rows] = lse_tile
            else:
                hi = lse_tile.astype(bf16).astype(f32)
                rest = lse_tile - hi
                mid = rest.astype(bf16).astype(f32)
                parts = [jnp.where(lane < 8, hi, rest - mid), mid]
                obuf[rows, pl.ds(QUERY_HEADS, LSE_ROWS), :] = (
                    jnp.concatenate(parts, axis=1).astype(bf16))
            return 0

        if pair == 0:
            lbuf[...] = jnp.zeros_like(lbuf)
        if n == batch:
            rows_step(0, 0)
        else:
            lax.fori_loop(0, n // batch, rows_step, 0)
        if (pair + 1) % (PAIRS // OUT_CHUNKS) == 0:
            o_send(pair // (PAIRS // OUT_CHUNKS))

    rbuf[me] = obuf[my_place]

    fresh = fresh_in[0].astype(f32)
    new_lse = jnp.zeros((GROUP, HEAD_WIDTH), f32)
    for head in range(KEY_VALUE_HEADS):
        cols = slice(head * HEAD_WIDTH, (head + 1) * HEAD_WIDTH)
        s = jnp.sum(own_q[head * GROUP:(head + 1) * GROUP] * fresh[0:1, cols],
                    axis=-1, keepdims=True) * SCALE
        new_lse = jnp.where(lane[0] == head, s, new_lse)

    for c in range(OUT_CHUNKS):
        o_wait(orecv, c)

    parts = rbuf[:, pl.ds(QUERY_HEADS, LSE_ROWS), :].astype(f32)
    hi = parts[:, :GROUP, :]
    mid = parts[:, GROUP:, :]
    lo = pltpu.roll(hi, HEAD_WIDTH - 8, 2)
    lse = (hi + mid) + lo
    top = jnp.maximum(jnp.max(lse, axis=0), new_lse)
    weights = jnp.exp(lse - top[None])
    new_weight = jnp.exp(new_lse - top)
    inverse = 1.0 / (jnp.sum(weights, axis=0) + new_weight)
    weights = weights * inverse[None]
    new_weight = new_weight * inverse
    outs = []
    for pair in range(PAIRS):
        tile = pl.ds(pair * TILE, TILE)
        blocks = rbuf[:, tile, :].astype(f32)
        for i in range(2):
            head = 2 * pair + i
            cols = slice(head * HEAD_WIDTH, (head + 1) * HEAD_WIDTH)
            part = blocks[:, i * GROUP:(i + 1) * GROUP, :]
            acc = jnp.sum(weights[:, :, head:head + 1] * part, axis=0)
            outs.append(acc + new_weight[:, head:head + 1] * fresh[1:2, cols])
    out_ref[...] = jnp.concatenate(outs, axis=0).reshape(out_ref.shape).astype(bf16)

    for c in range(QUERY_CHUNKS):
        q_wait(qsend, c)
        if c >= DIRECT:
            forward(c).wait_send()
    for c in range(OUT_CHUNKS):
        o_wait(osend, c)


def per_device(queries, prefix_key_value, suffix_key_value, fresh_key_value, lengths, home):
    n = lax.axis_size("blk")
    prefix = prefix_key_value.shape[1]
    slots = suffix_key_value.shape[2]
    width = KEY_VALUE_HEADS * HEAD_WIDTH
    bf16 = jnp.bfloat16
    flops = 4 * QUERY_HEADS * HEAD_WIDTH * (n * prefix + slots)
    out = pl.pallas_call(
        functools.partial(kernel, n),
        out_shape=jax.ShapeDtypeStruct(queries.shape, bf16),
        in_specs=[pl.BlockSpec(memory_space=pl.ANY)] * 6,
        out_specs=pl.BlockSpec(memory_space=pltpu.VMEM),
        scratch_shapes=[
            pltpu.SMEM(home.shape, jnp.int32),
            pltpu.SMEM(lengths.shape, jnp.int32),
            pltpu.VMEM(queries.shape, bf16),
            pltpu.VMEM(fresh_key_value.shape, bf16),
            pltpu.VMEM((n, QUERY_HEADS + LSE_ROWS, HEAD_WIDTH), bf16),
            pltpu.VMEM((n, QUERY_HEADS + LSE_ROWS, HEAD_WIDTH), bf16),
            pltpu.VMEM((n, GROUP, HEAD_WIDTH), jnp.float32),
            pltpu.VMEM((prefix, width), bf16),
            pltpu.VMEM((prefix, width), bf16),
            pltpu.VMEM((slots, width), bf16),
            pltpu.VMEM((slots, width), bf16),
            pltpu.SemaphoreType.DMA((8,)),
            pltpu.SemaphoreType.DMA((QUERY_CHUNKS,)),
            pltpu.SemaphoreType.DMA((QUERY_CHUNKS,)),
            pltpu.SemaphoreType.DMA((QUERY_CHUNKS,)),
            pltpu.SemaphoreType.DMA((QUERY_CHUNKS,)),
            pltpu.SemaphoreType.DMA((OUT_CHUNKS,)),
            pltpu.SemaphoreType.DMA((OUT_CHUNKS,)),
        ] + [
            pltpu.VMEM((n, QUERY_HEADS // QUERY_CHUNKS, HEAD_WIDTH), bf16)
        ] * QUERY_CHUNKS,
        compiler_params=pltpu.CompilerParams(
            collective_id=0, has_side_effects=True, vmem_limit_bytes=60 * 1024 * 1024
        ),
        cost_estimate=pl.CostEstimate(
            flops=flops, bytes_accessed=4 * width * (prefix + slots),
            transcendentals=QUERY_HEADS * n * prefix,
        ),
    )(home, lengths, queries, fresh_key_value, prefix_key_value, suffix_key_value)
    return out


def solution(mesh):
    placed = (
        P(("groups", "blk"), None),
        P(None, ("groups", "blk"), None),
        P(("groups", "blk"), None, None, None),
        P(("groups", "blk"), None, None),
        P("groups"),
        P("groups"),
    )
    return jax.shard_map(
        per_device,
        mesh=mesh,
        in_specs=placed,
        out_specs=P(("groups", "blk"), None),
        check_vma=False,
    )
```

```python
import functools

import jax
import jax.numpy as jnp
from jax import lax
from jax.experimental import pallas as pl
from jax.experimental.pallas import tpu as pltpu
from jax.sharding import PartitionSpec as P

QUERY_HEADS = 64
KEY_VALUE_HEADS = 8
HEAD_WIDTH = 128
GROUP = QUERY_HEADS // KEY_VALUE_HEADS
SCALE = HEAD_WIDTH ** (-0.5)
LOG2E = 1.4426950408889634
TILE = 2 * GROUP
PAIRS = KEY_VALUE_HEADS // 2
LSE_ROWS = 16
QUERY_CHUNKS = 4
OUT_CHUNKS = 4
MESH = pl.DeviceIdType.MESH


def each(last, body):
    if last <= 16:
        for k in range(last):
            body(k)
    else:
        def step(k, _):
            body(k)
            return 0

        lax.fori_loop(0, last, step, 0)


def kernel(n, home_ref, lengths_ref, q_ref, fresh_ref, prefix_ref, suffix_ref, out_ref,
           home, lengths, q_in, fresh_in, obuf, rbuf, lbuf, kbuf, vbuf, skbuf, svbuf,
           load_sem, qsend, qrecv, osend, orecv, *qbufs):
    me = lax.axis_index("blk")
    f32, bf16 = jnp.float32, jnp.bfloat16

    def peer_of(k):
        return k + jnp.where(k >= me, 1, 0)

    loads = [
        pltpu.make_async_copy(q_ref, q_in, load_sem.at[0]),
        pltpu.make_async_copy(home_ref, home, load_sem.at[1]),
        pltpu.make_async_copy(lengths_ref, lengths, load_sem.at[2]),
        pltpu.make_async_copy(prefix_ref.at[0], kbuf, load_sem.at[3]),
        pltpu.make_async_copy(suffix_ref.at[0, 0], skbuf, load_sem.at[4]),
        pltpu.make_async_copy(prefix_ref.at[1], vbuf, load_sem.at[5]),
        pltpu.make_async_copy(suffix_ref.at[0, 1], svbuf, load_sem.at[6]),
        pltpu.make_async_copy(fresh_ref, fresh_in, load_sem.at[7]),
    ]

    barrier = pltpu.get_barrier_semaphore()

    def greet(k):
        pl.semaphore_signal(barrier, inc=1, device_id={"blk": peer_of(k)}, device_id_type=MESH)

    loads[0].start()
    each(n - 1, greet)
    for load in loads[1:]:
        load.start()

    q_rows = QUERY_HEADS // QUERY_CHUNKS
    loads[0].wait()
    own_q = q_in[...].astype(f32).reshape(QUERY_HEADS, HEAD_WIDTH)
    for c in range(QUERY_CHUNKS):
        qbufs[c][me] = own_q[c * q_rows:(c + 1) * q_rows].astype(bf16)

    pl.semaphore_wait(barrier, n - 1)

    for c in range(QUERY_CHUNKS):
        def q_send(k, c=c):
            pltpu.make_async_remote_copy(
                src_ref=qbufs[c].at[me], dst_ref=qbufs[c].at[me],
                send_sem=qsend.at[c], recv_sem=qrecv.at[c],
                device_id={"blk": peer_of(n - 2 - k)}, device_id_type=MESH,
            ).start()

        each(n - 1, q_send)

    loads[1].wait()
    loads[2].wait()

    def find(r, carry):
        row, length = carry
        here = home[r] == me
        return jnp.where(here, r, row), jnp.where(here, lengths[r], length)

    slot_row, slot_len = lax.fori_loop(0, n, find, (jnp.int32(0), jnp.int32(0)))

    def q_wait(sem, c):
        part = qbufs[c].at[pl.ds(0, n - 1)]
        pltpu.make_async_copy(part, part, sem.at[c]).wait()

    o_rows = QUERY_HEADS // OUT_CHUNKS

    def o_span(c):
        extra = LSE_ROWS if c == OUT_CHUNKS - 1 else 0
        return pl.ds(c * o_rows, o_rows + extra)

    def o_send(c):
        rows = o_span(c)

        def body(k):
            peer = peer_of(k)
            pltpu.make_async_remote_copy(
                src_ref=obuf.at[peer, rows], dst_ref=rbuf.at[me, rows],
                send_sem=osend.at[c], recv_sem=orecv.at[c],
                device_id={"blk": peer}, device_id_type=MESH,
            ).start()

        each(n - 1, body)

    def o_wait(sem, c):
        part = rbuf.at[pl.ds(0, n - 1), o_span(c)]
        pltpu.make_async_copy(part, part, sem.at[c]).wait()

    batch = 16 if n % 16 == 0 else n
    live = lax.broadcasted_iota(jnp.int32, (GROUP, skbuf.shape[0]), 1) < slot_len
    lane = lax.broadcasted_iota(jnp.int32, (1, 1, HEAD_WIDTH), 2)
    row_id = lax.broadcasted_iota(jnp.int32, (batch, 1, 1), 0)
    nt = (((1,), (1,)), ((), ()))

    def softmax_part(scores, values):
        peak = jnp.max(scores, axis=-1, keepdims=True)
        p = jnp.exp2((scores - peak) * (SCALE * LOG2E))
        total = jnp.sum(p, axis=-1, keepdims=True)
        acc = jnp.dot(p.astype(bf16), values, preferred_element_type=f32)
        return peak, total, acc

    for pair in range(PAIRS):
        if pair % (PAIRS // QUERY_CHUNKS) == 0:
            q_wait(qrecv, pair // (PAIRS // QUERY_CHUNKS))
        if pair == 0:
            for load in loads[3:]:
                load.wait()
        tile = pl.ds(pair * TILE, TILE)
        qbuf = qbufs[pair // (PAIRS // QUERY_CHUNKS)]
        q_tile = pl.ds(pair % (PAIRS // QUERY_CHUNKS) * TILE, TILE)
        slot_q = qbuf[slot_row, q_tile, :].astype(f32)
        suffix = []
        for i in range(2):
            cols = pl.ds((2 * pair + i) * HEAD_WIDTH, HEAD_WIDTH)
            q = slot_q[i * GROUP:(i + 1) * GROUP].astype(bf16)
            s = lax.dot_general(q, skbuf[:, cols], nt, preferred_element_type=f32)
            s = jnp.where(live, s, -jnp.inf)
            suffix.append(softmax_part(s, svbuf[:, cols]))

        def rows_step(b, _, pair=pair, tile=tile, suffix=suffix, qbuf=qbuf, q_tile=q_tile):
            rows = pl.ds(b * batch, batch)
            is_slot = row_id + b * batch == slot_row
            q_all = qbuf[rows, q_tile, :].astype(f32)
            outs = []
            lse_tile = lbuf[rows]
            for i in range(2):
                head = 2 * pair + i
                cols = pl.ds(head * HEAD_WIDTH, HEAD_WIDTH)
                q = q_all[:, i * GROUP:(i + 1) * GROUP, :].reshape(batch * GROUP, HEAD_WIDTH)
                s = lax.dot_general(q.astype(bf16), kbuf[:, cols], nt, preferred_element_type=f32)
                m_p, l_p, a_p = softmax_part(s, vbuf[:, cols])
                m_p = m_p.reshape(batch, GROUP, 1)
                l_p = l_p.reshape(batch, GROUP, 1)
                a_p = a_p.reshape(batch, GROUP, HEAD_WIDTH)
                m_s, l_s, a_s = suffix[i]
                m_s = jnp.where(is_slot, m_s[None], -jnp.inf)
                peak = jnp.maximum(m_p, m_s)
                f_p = jnp.exp2((m_p - peak) * (SCALE * LOG2E))
                f_s = jnp.exp2((m_s - peak) * (SCALE * LOG2E))
                total = f_p * l_p + f_s * l_s[None]
                inverse = 1.0 / total
                outs.append((f_p * inverse) * a_p + (f_s * inverse) * a_s[None])
                lse = peak * SCALE + jnp.log(total)
                lse_tile = jnp.where(lax.rem(lane, 8) == head, lse, lse_tile)
            obuf[rows, tile, :] = jnp.concatenate(outs, axis=1).astype(bf16)
            if pair < PAIRS - 1:
                lbuf[rows] = lse_tile
            else:
                hi = lse_tile.astype(bf16).astype(f32)
                rest = lse_tile - hi
                mid = rest.astype(bf16).astype(f32)
                parts = [jnp.where(lane < 8, hi, rest - mid), mid]
                obuf[rows, pl.ds(QUERY_HEADS, LSE_ROWS), :] = (
                    jnp.concatenate(parts, axis=1).astype(bf16))
            return 0

        if pair == 0:
            lbuf[...] = jnp.zeros_like(lbuf)
        if n == batch:
            rows_step(0, 0)
        else:
            lax.fori_loop(0, n // batch, rows_step, 0)
        if (pair + 1) % (PAIRS // OUT_CHUNKS) == 0:
            o_send(pair // (PAIRS // OUT_CHUNKS))

    rbuf[me] = obuf[me]

    fresh = fresh_in[0].astype(f32)
    new_lse = jnp.zeros((GROUP, HEAD_WIDTH), f32)
    for head in range(KEY_VALUE_HEADS):
        cols = slice(head * HEAD_WIDTH, (head + 1) * HEAD_WIDTH)
        s = jnp.sum(own_q[head * GROUP:(head + 1) * GROUP] * fresh[0:1, cols],
                    axis=-1, keepdims=True) * SCALE
        new_lse = jnp.where(lane[0] == head, s, new_lse)

    for c in range(OUT_CHUNKS):
        o_wait(orecv, c)

    parts = rbuf[:, pl.ds(QUERY_HEADS, LSE_ROWS), :].astype(f32)
    hi = parts[:, :GROUP, :]
    mid = parts[:, GROUP:, :]
    lo = pltpu.roll(hi, HEAD_WIDTH - 8, 2)
    lse = (hi + mid) + lo
    top = jnp.maximum(jnp.max(lse, axis=0), new_lse)
    weights = jnp.exp(lse - top[None])
    new_weight = jnp.exp(new_lse - top)
    inverse = 1.0 / (jnp.sum(weights, axis=0) + new_weight)
    weights = weights * inverse[None]
    new_weight = new_weight * inverse
    outs = []
    for pair in range(PAIRS):
        tile = pl.ds(pair * TILE, TILE)
        blocks = rbuf[:, tile, :].astype(f32)
        for i in range(2):
            head = 2 * pair + i
            cols = slice(head * HEAD_WIDTH, (head + 1) * HEAD_WIDTH)
            part = blocks[:, i * GROUP:(i + 1) * GROUP, :]
            acc = jnp.sum(weights[:, :, head:head + 1] * part, axis=0)
            outs.append(acc + new_weight[:, head:head + 1] * fresh[1:2, cols])
    out_ref[...] = jnp.concatenate(outs, axis=0).reshape(out_ref.shape).astype(bf16)

    for c in range(QUERY_CHUNKS):
        q_wait(qsend, c)
    for c in range(OUT_CHUNKS):
        o_wait(osend, c)


def per_device(queries, prefix_key_value, suffix_key_value, fresh_key_value, lengths, home):
    n = lax.axis_size("blk")
    prefix = prefix_key_value.shape[1]
    slots = suffix_key_value.shape[2]
    width = KEY_VALUE_HEADS * HEAD_WIDTH
    bf16 = jnp.bfloat16
    flops = 4 * QUERY_HEADS * HEAD_WIDTH * (n * prefix + slots)
    out = pl.pallas_call(
        functools.partial(kernel, n),
        out_shape=jax.ShapeDtypeStruct(queries.shape, bf16),
        in_specs=[pl.BlockSpec(memory_space=pl.ANY)] * 6,
        out_specs=pl.BlockSpec(memory_space=pltpu.VMEM),
        scratch_shapes=[
            pltpu.SMEM(home.shape, jnp.int32),
            pltpu.SMEM(lengths.shape, jnp.int32),
            pltpu.VMEM(queries.shape, bf16),
            pltpu.VMEM(fresh_key_value.shape, bf16),
            pltpu.VMEM((n, QUERY_HEADS + LSE_ROWS, HEAD_WIDTH), bf16),
            pltpu.VMEM((n, QUERY_HEADS + LSE_ROWS, HEAD_WIDTH), bf16),
            pltpu.VMEM((n, GROUP, HEAD_WIDTH), jnp.float32),
            pltpu.VMEM((prefix, width), bf16),
            pltpu.VMEM((prefix, width), bf16),
            pltpu.VMEM((slots, width), bf16),
            pltpu.VMEM((slots, width), bf16),
            pltpu.SemaphoreType.DMA((8,)),
            pltpu.SemaphoreType.DMA((QUERY_CHUNKS,)),
            pltpu.SemaphoreType.DMA((QUERY_CHUNKS,)),
            pltpu.SemaphoreType.DMA((OUT_CHUNKS,)),
            pltpu.SemaphoreType.DMA((OUT_CHUNKS,)),
        ] + [
            pltpu.VMEM((n, QUERY_HEADS // QUERY_CHUNKS, HEAD_WIDTH), bf16)
        ] * QUERY_CHUNKS,
        compiler_params=pltpu.CompilerParams(
            collective_id=0, has_side_effects=True, vmem_limit_bytes=60 * 1024 * 1024
        ),
        cost_estimate=pl.CostEstimate(
            flops=flops, bytes_accessed=4 * width * (prefix + slots),
            transcendentals=QUERY_HEADS * n * prefix,
        ),
    )(home, lengths, queries, fresh_key_value, prefix_key_value, suffix_key_value)
    return out


def solution(mesh):
    placed = (
        P(("groups", "blk"), None),
        P(None, ("groups", "blk"), None),
        P(("groups", "blk"), None, None, None),
        P(("groups", "blk"), None, None),
        P("groups"),
        P("groups"),
    )
    return jax.shard_map(
        per_device,
        mesh=mesh,
        in_specs=placed,
        out_specs=P(("groups", "blk"), None),
        check_vma=False,
    )
```
